32 devices in a mesh: dp: 8 (over y, x, core), tensor: 4 (over z).
Axes of the slice: x: 2, y: 2, z: 4, core: 2. Of those that a mesh axis runs over, the one named last changes fastest.
Arguments:
- tokens: bfloat16 [8192, 768], P('dp'), may hold values from -6 to 6
- cotangent: bfloat16 [8192, 768], P('dp'), may hold values from -6 to 6
- kept_counts: int32 [16], P('dp'), may hold values from 98 to 576, as said below
- patch_pos: int32 [2, 8192], P(None, 'dp'), may hold values from 0 to 23, as said below
- attn_norm_gain: float32 [768], replicated, may hold values from 0.5 to 1.5
- attn_norm_bias: float32 [768], replicated, may hold values from -1.75 to 1.75
- qkv_weight: bfloat16 [768, 3, 768], P(None, None, 'tensor'), may hold values from -0.21875 to 0.21875
- qkv_bias: float32 [3, 768], P(None, 'tensor'), may hold values from -1.75 to 1.75
- rope_freq: float32 [2, 384], P(None, 'tensor'), may hold values from -3 to 3
- out_weight: bfloat16 [768, 768], P('tensor'), may hold values from -2 to 2
- out_bias: float32 [768], replicated, may hold values from -1.75 to 1.75
- mlp_norm_gain: float32 [768], replicated, may hold values from 0.5 to 1.5
- mlp_norm_bias: float32 [768], replicated, may hold values from -1.75 to 1.75
- up_weight: bfloat16 [768, 3072], P(None, 'tensor'), may hold values from -0.21875 to 0.21875
- up_bias: float32 [3072], P('tensor'), may hold values from -1.75 to 1.75
- down_weight: bfloat16 [3072, 768], P('tensor'), may hold values from -0.109375 to 0.109375
- down_bias: float32 [768], replicated, may hold values from -1.75 to 1.75
Outputs:
- block_out: bfloat16 [8192, 768], P('dp')
- grad_tokens: bfloat16 [8192, 768], P('dp')
- grad_attn_gain: float32 [768], replicated
- grad_attn_bias: float32 [768], replicated
- grad_qkv_weight: float32 [768, 3, 768], P(None, None, 'tensor')
- grad_qkv_bias: float32 [3, 768], P(None, 'tensor')
- grad_rope_freq: float32 [2, 384], P(None, 'tensor')
- grad_out_weight: float32 [768, 768], P('tensor')
- grad_out_bias: float32 [768], replicated
- grad_mlp_gain: float32 [768], replicated
- grad_mlp_bias: float32 [768], replicated
- grad_up_weight: float32 [768, 3072], P(None, 'tensor')
- grad_up_bias: float32 [3072], P('tensor')
- grad_down_weight: float32 [3072, 768], P('tensor')
- grad_down_bias: float32 [768], replicated
The draws below stay inside these ranges and needn't reach their ends.
Inputs may be any that keep to these rules, and one draw needn't show every extreme that they name: `kept_counts`: entry d * 2 + i is the number of kept patches of image slot i of pack d; an image comes from a grid of 14 x 14 or 24 x 24 patches; the counts of one pack sum to at most 1024. `patch_pos`: row 0 holds each slot's patch row, row 1 its column, in its image's grid; the kept patches of one image have distinct positions; padding slots hold 0.
All inputs are finite; a program needn't handle non-finite values.
Results may differ from the reference program's by a relative error of at most 0.02.
Values may be sent and summed in bfloat16 or wider, within the bound.
A program may use at most 128 MiB of HBM per device.

```python
import jax
import jax.numpy as jnp
from jax import lax

D = 768
HEADS = 12
FF = 3072
HEAD_DIM = 64
IMG_DEV = 2
TOK_DEV = 1024
TOKENS = 8192
IMAGES = 16
N_TENSOR = 4


stride_table = (5, 11, 13, 17, 19, 23, 25, 29, 31, 37, 41, 43, 47, 53, 55, 59)


def packing(key):
    devices_count = IMAGES // IMG_DEV
    base_key = jax.random.fold_in(key, 7)
    keys_list = jax.random.split(base_key, 6)
    device_ids = jnp.arange(devices_count, dtype=jnp.int32)[:, None]
    image_ids = jnp.arange(IMG_DEV, dtype=jnp.int32)[None, :]
    is_large = jax.random.randint(keys_list[0], (devices_count, IMG_DEV), 0, 2)
    chosen = jax.random.randint(keys_list[1], (), 0, devices_count)
    forced = (device_ids == chosen) & (image_ids == 0)
    is_large = jnp.where(forced, 1, is_large)
    grid_side = jnp.where(is_large == 1, 24, 14)
    initial = grid_side * grid_side
    dropped = jax.random.randint(keys_list[2], (devices_count, IMG_DEV), 0, initial // 2 + 1)
    dropping = jax.random.randint(keys_list[3], (devices_count, IMG_DEV), 0, 2)
    dropped = jnp.where(forced, 0, dropped * dropping)
    kept_now = initial - dropped
    before = jnp.cumsum(kept_now, axis=1) - kept_now
    is_last = image_ids == IMG_DEV - 1
    kept_now = jnp.where(is_last, jnp.minimum(kept_now, TOK_DEV - before), kept_now)
    image_ends = jnp.cumsum(kept_now, axis=1)
    image_starts = image_ends - kept_now
    slot_ids = jnp.arange(TOK_DEV, dtype=jnp.int32)[None, :, None]
    owner_image = jnp.sum((slot_ids >= image_ends[:, None, :]).astype(jnp.int32), axis=2)
    filled = owner_image < IMG_DEV
    owner_safe = jnp.minimum(owner_image, IMG_DEV - 1)
    step_size = jnp.array(stride_table, dtype=jnp.int32)[jax.random.randint(keys_list[4], (devices_count, IMG_DEV), 0, 16)]
    offset = jax.random.randint(keys_list[5], (devices_count, IMG_DEV), 0, 576)

    def pick_owner(source_table):
        return jnp.take_along_axis(source_table, owner_safe, axis=1)
    local_slot = slot_ids[..., 0] - pick_owner(image_starts)
    side_now = pick_owner(grid_side)
    position = (local_slot * pick_owner(step_size) + pick_owner(offset)) % (side_now * side_now)
    row_ids = jnp.where(filled, position // side_now, 0)
    col_ids = jnp.where(filled, position % side_now, 0)
    return (kept_now.reshape(-1), jnp.stack([row_ids.reshape(-1), col_ids.reshape(-1)]))


def draw_kept_counts(key, part):
    return packing(key)[0].astype(jnp.int32)


def draw_patch_pos(key, part):
    return packing(key)[1].astype(jnp.int32)


def shard_levels(own_key, shape, pieces, low, top_value):
    gain, own = 1.0, jax.random.fold_in(own_key, 6)
    for dim, parts in pieces:
        heights = jnp.exp(jax.random.uniform(jax.random.fold_in(own, dim), (parts,), jnp.float32, low / len(pieces), top_value / len(pieces)))
        gain = gain * jnp.repeat(heights, shape[dim] // parts).reshape([-1 if axis == dim else 1 for axis in range(len(shape))])
    return gain


def noise(stream_key, shape, scale, limit, shards=(), held_as=jnp.bfloat16):
    entries = jax.random.normal(stream_key, shape, jnp.float32) * scale
    if len(shards) > 0:
        entries = shard_levels(stream_key, shape, shards, -0.22, 0.18) * entries
    return jnp.clip(entries, min=-limit, max=limit).astype(held_as)


def setup_inputs(seed: int = 0) -> dict:
    seeds = jax.random.split(jax.random.key(seed), 18)
    return {
        "tokens": noise(seeds[0], (TOKENS, D), 1.0, 6.0, ((0, 8),)),
        "cotangent": noise(seeds[1], (TOKENS, D), 1.0, 6.0, ((0, 8),)),
        "kept_counts": draw_kept_counts(jax.random.fold_in(seeds[17], 71), 0),
        "patch_pos": draw_patch_pos(jax.random.fold_in(seeds[17], 71), 0),
        "attn_norm_gain": jnp.clip(1.0 + 0.1 * jax.random.normal(seeds[4], (D,), jnp.float32), 0.5, 1.5),
        "attn_norm_bias": noise(seeds[5], (D,), 0.3, 1.75, (), jnp.float32),
        "qkv_weight": noise(seeds[6], (D, 3, D), D ** -0.5, 0.21875, ((2, 4),)),
        "qkv_bias": noise(seeds[7], (3, D), 0.3, 1.75, ((1, 4),), jnp.float32),
        "rope_freq": noise(seeds[8], (2, D // 2), 0.5, 3.0, ((1, 4),), jnp.float32),
        "out_weight": noise(seeds[9], (D, D), 8 ** -0.5, 2.0, ((0, 4),)),
        "out_bias": noise(seeds[10], (D,), 0.3, 1.75, (), jnp.float32),
        "mlp_norm_gain": jnp.clip(1.0 + 0.1 * jax.random.normal(seeds[11], (D,), jnp.float32), 0.5, 1.5),
        "mlp_norm_bias": noise(seeds[12], (D,), 0.3, 1.75, (), jnp.float32),
        "up_weight": noise(seeds[13], (D, FF), D ** -0.5, 0.21875, ((1, 4),)),
        "up_bias": noise(seeds[14], (FF,), 0.3, 1.75, ((0, 4),), jnp.float32),
        "down_weight": noise(seeds[15], (FF, D), FF ** -0.5, 0.109375, ((0, 4),)),
        "down_bias": noise(seeds[16], (D,), 0.3, 1.75, (), jnp.float32),
    }


@jax.custom_vjp
def low(v):
    return lax.optimization_barrier(v.astype(jnp.bfloat16)).astype(jnp.float32)

@jax.custom_vjp
def low_back(v):
    return v

def low_keep(v):
    return (low(v), None)

def low_pass(kept, grad):
    return (grad,)

def back_keep(v):
    return (v, None)

def back_low(kept, grad):
    return (low(grad),)
low.defvjp(low_keep, low_pass)
low_back.defvjp(back_keep, back_low)
highest = lax.Precision.HIGHEST

def norm_rows(values, norm_gain, norm_shift):
    mean_val = lax.optimization_barrier(jnp.mean(values, axis=-1, keepdims=True))
    centered = values - mean_val
    spread = lax.optimization_barrier(jnp.mean(centered * centered, axis=-1, keepdims=True))
    return centered * lax.rsqrt(spread + 1e-06) * norm_gain + norm_shift

def rotate(values, cosine, sine_val):
    half_dim = values.shape[-1] // 2
    first_half = values[..., :half_dim]
    second_half = values[..., half_dim:]
    return jnp.concatenate([first_half * cosine - second_half * sine_val, first_half * sine_val + second_half * cosine], axis=-1)

def attend(query_in, key_in, value_in, segment):
    row_count, head_count, head_width = query_in.shape
    block_span = min(512, row_count)
    block_count = row_count // block_span
    score_scale = head_width ** (-0.5)

    def one_block(block_pair):
        query_block, segment_block = block_pair
        scores = jnp.einsum('qhd,khd->hqk', query_block, key_in, precision=highest) * score_scale
        scores = low_back(scores)
        same_image = segment_block[:, None] == segment[None, :]
        scores = jnp.where(same_image[None], scores, -1e+30)
        row_peak = lax.optimization_barrier(jnp.max(scores, axis=-1, keepdims=True))
        row_exp = jnp.exp(scores - row_peak)
        prob_low = low(row_exp / lax.optimization_barrier(jnp.sum(row_exp, axis=-1, keepdims=True)))
        return jnp.einsum('hqk,khd->qhd', prob_low, value_in, precision=highest)
    block_outs = lax.map(jax.checkpoint(one_block), (query_in.reshape(block_count, block_span, head_count, head_width), segment.reshape(block_count, block_span)))
    return block_outs.reshape(row_count, head_count, head_width)

def block_layer(inputs, weights_all, segment, alive_rows, row_float, col_float):
    attn_gain, attn_shift, qkv_all, qkv_shift, freq_all, out_all, out_shift, mlp_gain, mlp_shift, up_all, up_shift, down_all, down_shift = weights_all
    row_count = inputs.shape[0]
    heads_here = HEADS // N_TENSOR
    columns = heads_here * HEAD_DIM
    half_dim = HEAD_DIM // 2
    units_here = FF // N_TENSOR
    attn_input = low(norm_rows(inputs, attn_gain, attn_shift))
    head_sum = jnp.zeros((row_count, D), jnp.float32)
    for group_index in range(N_TENSOR):
        input_part = low_back(attn_input)
        col_lo = group_index * columns
        weight_part = qkv_all[:, :, col_lo:col_lo + columns].reshape(D, 3 * columns)
        projected = jnp.dot(input_part, weight_part, precision=highest) + qkv_shift[:, col_lo:col_lo + columns].reshape(3 * columns)
        projected = low_back(projected).reshape(row_count, 3, heads_here, HEAD_DIM)
        freq_lo = group_index * heads_here * half_dim
        freq_part = freq_all[:, freq_lo:freq_lo + heads_here * half_dim].reshape(2, heads_here, half_dim)
        angles = row_float[:, None, None] * freq_part[0][None] + col_float[:, None, None] * freq_part[1][None]
        cosine = jnp.cos(angles)
        sine_val = jnp.sin(angles)
        query_low = low(rotate(projected[:, 0], cosine, sine_val))
        key_low = low(rotate(projected[:, 1], cosine, sine_val))
        value_low = low(projected[:, 2])
        mixed_heads = attend(query_low, key_low, value_low, segment)
        mixed_heads = low(low_back(mixed_heads)).reshape(row_count, columns)
        head_sum = head_sum + low(low_back(jnp.dot(mixed_heads, out_all[col_lo:col_lo + columns], precision=highest)))
    hidden = inputs + head_sum + out_shift
    mlp_input = low(norm_rows(hidden, mlp_gain, mlp_shift))
    unit_sum = jnp.zeros((row_count, D), jnp.float32)
    for group_index in range(N_TENSOR):
        input_part = low_back(mlp_input)
        unit_lo = group_index * units_here
        upward = jnp.dot(input_part, up_all[:, unit_lo:unit_lo + units_here], precision=highest) + up_shift[unit_lo:unit_lo + units_here]
        upward = low_back(upward)
        activ = low(jax.nn.gelu(upward, approximate=False))
        unit_sum = unit_sum + low(low_back(jnp.dot(activ, down_all[unit_lo:unit_lo + units_here], precision=highest)))
    return alive_rows[:, None] * (hidden + unit_sum + down_shift)

def segments_of(counts, row_count):
    image_ends = jnp.cumsum(counts, dtype=jnp.int32)
    position = jnp.arange(row_count, dtype=jnp.int32)
    return lax.optimization_barrier(jnp.sum((position[:, None] >= image_ends[None, :]).astype(jnp.int32), axis=1, dtype=jnp.int32))

def reference(tokens, cotangent, kept_counts, patch_pos, attn_norm_gain, attn_norm_bias, qkv_weight, qkv_bias, rope_freq, out_weight, out_bias, mlp_norm_gain, mlp_norm_bias, up_weight, up_bias, down_weight, down_bias):
    pack_count = tokens.shape[0] // TOK_DEV
    inputs_all = tokens.astype(jnp.float32).reshape(pack_count, TOK_DEV, D)
    grads_in = cotangent.astype(jnp.float32).reshape(pack_count, TOK_DEV, D)
    counts_all = kept_counts.reshape(pack_count, IMG_DEV)
    rows_all = patch_pos[0].reshape(pack_count, TOK_DEV)
    cols_all = patch_pos[1].reshape(pack_count, TOK_DEV)
    weights_all = tuple((item_arr.astype(jnp.float32) for item_arr in (attn_norm_gain, attn_norm_bias, qkv_weight, qkv_bias, rope_freq, out_weight, out_bias, mlp_norm_gain, mlp_norm_bias, up_weight, up_bias, down_weight, down_bias)))

    def one_pack(running, pack_data):
        pack_inputs, pack_grads, pack_counts, pack_rows, pack_cols = pack_data
        segment = segments_of(pack_counts, TOK_DEV)
        alive_rows = (segment < IMG_DEV).astype(jnp.float32)
        row_float = pack_rows.astype(jnp.float32)
        col_float = pack_cols.astype(jnp.float32)

        def forward(inputs, weights_now):
            return block_layer(inputs, weights_now, segment, alive_rows, row_float, col_float)
        pack_out, pullback = jax.vjp(forward, pack_inputs, weights_all)
        grad_pack, grad_weights = pullback(pack_grads)
        running = jax.tree.map(lambda summed, added: summed + added, running, grad_weights)
        return (running, (pack_out, grad_pack))
    zero_sums = jax.tree.map(jnp.zeros_like, weights_all)
    totals, (pack_outs, pack_grads_all) = lax.scan(one_pack, zero_sums, (inputs_all, grads_in, counts_all, rows_all, cols_all))
    return (pack_outs.reshape(-1, D).astype(jnp.bfloat16), pack_grads_all.reshape(-1, D).astype(jnp.bfloat16), totals[0], totals[1], totals[2], totals[3], totals[4], totals[5], totals[6], totals[7], totals[8], totals[9], totals[10], totals[11], totals[12])
```

```python
import functools

import jax
import jax.numpy as jnp
from jax import lax
from jax.experimental import pallas as pl
from jax.experimental.pallas import tpu as pltpu
from jax.sharding import PartitionSpec as P

HEAD_DIM = 64
HALF = HEAD_DIM // 2
GRID_SIDE = 24
EPS = 1e-06
BIG = 1e30
F32 = jnp.float32
BF16 = jnp.bfloat16
NN = (((1,), (0,)), ((), ()))
NT = (((1,), (1,)), ((), ()))
TN = (((0,), (0,)), ((), ()))
VMEM = pl.BlockSpec(memory_space=pltpu.VMEM)
SMEM = pl.BlockSpec(memory_space=pltpu.SMEM)
ANY = pl.BlockSpec(memory_space=pl.ANY)
MESH = pl.DeviceIdType.MESH
TABLE_ROWS = 32
PEERS = 8
PARAMS = pltpu.CompilerParams(vmem_limit_bytes=60 * 1024 * 1024)


def dot(a, b, dims):
    return lax.dot_general(a, b, dims, preferred_element_type=F32)


def lanes(shape):
    return lax.broadcasted_iota(jnp.int32, shape, len(shape) - 1)


def norm_rows(values):
    center = values - jnp.mean(values, axis=-1, keepdims=True)
    inverse = lax.rsqrt(jnp.mean(center * center, axis=-1, keepdims=True) + EPS)
    return center * inverse, inverse


def norm_back(grad_out, scaled, inverse, gain):
    grad_scaled = grad_out * gain
    inner = jnp.mean(grad_scaled, axis=-1, keepdims=True)
    along = jnp.mean(grad_scaled * scaled, axis=-1, keepdims=True)
    return inverse * (grad_scaled - inner - scaled * along)


def swap_halves(u):
    first = lanes(u.shape) % HEAD_DIM < HALF
    return jnp.where(first, pltpu.roll(u, 128 - HALF, 1), pltpu.roll(u, HALF, 1))


def split3(v):
    high = v.astype(BF16)
    rest = v - high.astype(F32)
    mid = rest.astype(BF16)
    low = (rest - mid.astype(F32)).astype(BF16)
    return high, mid, low


def gelu_parts(v):
    x = jnp.abs(v) * 0.7071067811865476
    t = 1.0 / (1.0 + 0.3275911 * x)
    e = jnp.exp(-(x * x))
    poly = t * (
        0.254829592
        + t * (-0.284496736 + t * (1.421413741 + t * (-1.453152027 + t * 1.061405429)))
    )
    tail = 0.5 * poly * e
    phi = jnp.where(v >= 0, 1.0 - tail, tail)
    return phi, e * 0.3989422804014327


ROWS = 512
KEYS = 256


def even_lanes(shape):
    return lanes(shape) < HEAD_DIM


def rotary(meta, tab, m, rows, count):
    lane = lanes((count, 128))
    parts = []
    for axis in range(2):
        p = meta[rows, axis : axis + 1]
        hot = (lane == p) | (lane == p + TABLE_ROWS) | (lane == p + 2 * TABLE_ROWS)
        parts.append(dot(hot.astype(F32).astype(BF16), tab[m, axis], NN))
    rc, rs = parts[0][:, :256], parts[0][:, 256:]
    cc, sc = parts[1][:, :256], parts[1][:, 256:]
    cosine = rc * cc - rs * sc
    sine = rs * cc + rc * sc
    sine = jnp.where(lanes(sine.shape) % HEAD_DIM < HALF, -sine, sine)
    return cosine, sine


def row_block(i):
    return pl.ds(pl.multiple_of(i * ROWS, ROWS), ROWS)


class Places:
    def __init__(self):
        d, t = lax.axis_index("dp"), lax.axis_index("tensor")
        self.d, self.t = d, t
        low = d % PEERS
        b0, b1, b2 = low % 2, (low // 2) % 2, low // 4
        core, across_x, across_y = 1 - 2 * b0, 2 - 4 * b1, 4 - 8 * b2
        t0, t1 = t % 2, (t // 2) % 2
        flip0, flip1 = 1 - 2 * t0, 2 - 4 * t1
        self.slice = low
        self.slice_x, self.slice_y = low + across_x, low + across_y
        self.slice_xy = low + across_x + across_y
        self.core_step = core
        self.half = b0
        self.core = (d + core, t)
        self.x = (d + across_x, t)
        self.y = (d + across_y, t)
        self.xy = (d + across_x + across_y, t)
        self.z = [None, (d, t + flip0), (d, t + flip1), (d, t + flip0 + flip1)]


def greet(partners):
    barrier = pltpu.get_barrier_semaphore()
    for p in partners:
        pl.semaphore_signal(barrier, inc=1, device_id=p, device_id_type=MESH)
    pl.semaphore_wait(barrier, len(partners))


class Mail:
    def __init__(self, send_sem, recv_sem):
        self.send_sem, self.recv_sem = send_sem, recv_sem
        self.count = 0
        self.sent = []

    def number(self):
        self.count += 1
        return self.count - 1

    def send(self, n, src, dst, device):
        copy = pltpu.make_async_remote_copy(
            src_ref=src, dst_ref=dst, send_sem=self.send_sem.at[n], recv_sem=self.recv_sem.at[n],
            device_id=device, device_id_type=MESH,
        )
        copy.start()
        self.sent.append(copy)

    def arrive(self, n, dst, device):
        pltpu.make_async_remote_copy(
            src_ref=dst, dst_ref=dst, send_sem=self.send_sem.at[n], recv_sem=self.recv_sem.at[n],
            device_id=device, device_id_type=MESH,
        ).wait_recv()

    def finish(self):
        for copy in self.sent:
            copy.wait_send()


class Sliced:
    def __init__(self, mail, me, sources, targets, view, height):
        self.mail, self.me, self.view, self.height = mail, me, view, height
        self.transfers = targets
        self.z = [mail.number() for _ in targets]
        self.n = [mail.number() for _ in range(8)]

    def piece(self, s, off=0, size=None):
        size = self.height if size is None else size
        return self.view(pl.ds(pl.multiple_of(s * self.height + off, 16), size))

    def stage(self, k):
        mail, me, n = self.mail, self.me, self.n
        half = self.height // 2
        mine, sx, sy, sxy = me.slice, me.slice_x, me.slice_y, me.slice_xy
        if k == 0:
            for i, (device, source, landing) in zip(self.z, self.transfers):
                rows = pl.ds(pl.multiple_of(mine * self.height, 16), self.height)
                mail.send(i, source(rows), landing(rows), device)
        elif k == 1:
            for i, (device, source, landing) in zip(self.z, self.transfers):
                rows = pl.ds(pl.multiple_of(mine * self.height, 16), self.height)
                mail.arrive(i, landing(rows), device)
            mail.send(n[0], self.piece(mine), self.piece(mine), me.x)
            mail.send(n[1], self.piece(mine), self.piece(mine), me.y)
            mail.send(n[2], self.piece(mine), self.piece(mine), me.core)
        elif k == 2:
            mail.arrive(n[0], self.piece(sx), me.x)
            mail.send(n[3], self.piece(sx, 0, half), self.piece(sx, 0, half), me.y)
            mail.send(n[5], self.piece(sx), self.piece(sx), me.core)
            mail.arrive(n[1], self.piece(sy), me.y)
            mail.send(n[4], self.piece(sy, half, half), self.piece(sy, half, half), me.x)
            mail.send(n[6], self.piece(sy), self.piece(sy), me.core)
        elif k == 3:
            mail.arrive(n[3], self.piece(sxy, 0, half), me.y)
            mail.arrive(n[4], self.piece(sxy, half, half), me.x)
            mail.send(n[7], self.piece(sxy), self.piece(sxy), me.core)
        else:
            for i, s in ((2, mine), (5, sx), (6, sy), (7, sxy)):
                mail.arrive(n[i], self.piece(s + me.core_step), me.core)


class Direct:
    def __init__(self, mail, me, device, source, landing, height):
        self.mail, self.me = mail, me
        self.device, self.source, self.landing, self.height = device, source, landing, height
        self.n = [mail.number(), mail.number()]

    def stage(self, k):
        mail, me = self.mail, self.me
        mine = pl.ds(pl.multiple_of(me.half * self.height, 16), self.height)
        other = pl.ds(pl.multiple_of((1 - me.half) * self.height, 16), self.height)
        if k == 0:
            mail.send(self.n[0], self.source(mine), self.landing(mine), self.device)
        elif k == 1:
            mail.arrive(self.n[0], self.landing(mine), self.device)
            mail.send(self.n[1], self.landing(mine), self.landing(mine), me.core)
        else:
            mail.arrive(self.n[1], self.landing(other), me.core)


FRONT_MESSAGES = 80


def front_body(
    groups, tok, posr, counts, gain1, shift1, pack, ob, gain2, shift2, db,
    cot_in, wq_in, wo_in, wu_in, wd_in,
    qa_out, ka_out, va_out, do_out, out_out, gh_out, x_out, wq_out, tab_out, meta, dwo, dwu, dwd, sums,
    wq, wo, wud, pk, tab, flipped, cot, x, qa, ka, va, mixed, hidden, x2, unit_acc, grad_acc, dos, out,
    w_sem, s_sem, o_sem, send_sem, recv_sem,
):
    total = tok.shape[0]
    cols = wo_in.shape[0]
    width = tok.shape[1]
    steps = total // ROWS
    me = Places()
    mail = Mail(send_sem, recv_sem)
    lift = 256 - cols
    loads = [
        pltpu.make_async_copy(wq_in, wq.at[0], w_sem.at[0]),
        pltpu.make_async_copy(cot_in, cot, w_sem.at[1]),
        pltpu.make_async_copy(wo_in, wo.at[0, pl.ds(lift, cols), :], w_sem.at[2]),
        pltpu.make_async_copy(wu_in, wud.at[0, 0], w_sem.at[3]),
        pltpu.make_async_copy(wd_in, wud.at[0, 1], w_sem.at[4]),
    ]
    for c in loads:
        c.start()
    pack_numbers = [mail.number() for _ in range(groups - 1)]
    q1 = Direct(mail, me, me.z[1], lambda r: wq_in.at[r, :], lambda r: wq.at[1, r, :], width // 2)
    qh = width // PEERS
    qn = {
        m: Sliced(
            mail, me, None, [(me.z[m], lambda r: wq_in.at[r, :], lambda r, m=m: wq.at[m, r, :])],
            lambda r, m=m: wq.at[m, r, :], qh,
        )
        for m in range(2, groups)
    }
    oc = Sliced(
        mail, me, None,
        [(me.z[m], lambda r: wo.at[0, r, :], lambda r, m=m: wo.at[m, r, :]) for m in range(1, groups)],
        lambda r: wo.at[pl.ds(1, groups - 1), r, :], 256 // PEERS,
    )
    ud = {
        m: Sliced(
            mail, me, None,
            [
                (me.z[m], lambda r: wu_in.at[r, :], lambda r, m=m: wud.at[m, 0, r, :]),
                (me.z[m], lambda r: wd_in.at[r, :], lambda r, m=m: wud.at[m, 1, r, :]),
            ],
            lambda r, m=m: wud.at[m, :, r, :], width // PEERS,
        )
        for m in range(1, groups)
    }
    wo[0, 0:lift, :] = jnp.zeros((lift, width), BF16)
    greet(me.z[1:] + [me.core, me.x, me.y])
    for m in range(1, groups):
        mail.send(pack_numbers[m - 1], pack, pk.at[m], me.z[m])
    q1.stage(0)
    pk[0] = pack[...]

    flipped[...] = jnp.zeros_like(flipped)
    flipped[0:2, :] = posr[...].astype(F32)
    place = lax.broadcasted_iota(jnp.int32, (total, 8), 0)
    end = counts[0]
    segment = (place >= end).astype(jnp.int32)
    for n in range(1, counts.shape[0]):
        end = end + counts[n]
        segment += (place >= end).astype(jnp.int32)
    alive = (place < end).astype(jnp.int32)
    lane8 = lanes((total, 8))
    meta[...] = jnp.where(
        lane8 == 2, segment, jnp.where(lane8 == 3, alive, jnp.transpose(flipped[...]).astype(jnp.int32))
    )

    def make_table(m):
        place = lax.broadcasted_iota(jnp.int32, (TABLE_ROWS, 256), 0).astype(F32)
        for axis in range(2):
            angle = place * pk[m, 2 + axis : 3 + axis, 0:256]
            for n, part in enumerate(split3(jnp.concatenate([jnp.cos(angle), jnp.sin(angle)], axis=1))):
                tab[m, axis, TABLE_ROWS * n : TABLE_ROWS * (n + 1), :] = part
            tab[m, axis, 3 * TABLE_ROWS :, :] = jnp.zeros((128 - 3 * TABLE_ROWS, 512), BF16)

    make_table(0)
    for i in range(steps):
        rows = pl.ds(i * ROWS, ROWS)
        scaled, _ = norm_rows(tok[rows, :].astype(F32))
        x[rows, :] = (scaled * gain1[...] + shift1[...]).astype(BF16)
    for m in range(2, groups):
        qn[m].stage(0)
    x_store = pltpu.make_async_copy(x, x_out, s_sem.at[0, 3])
    x_store.start()

    def saves(m, slot):
        return [
            pltpu.make_async_copy(a.at[slot], b.at[m], s_sem.at[slot, n])
            for n, (a, b) in enumerate(((qa, qa_out), (ka, ka_out), (va, va_out)))
        ]

    def project(m, slot, i):
        rows = pl.ds(i * ROWS, ROWS)
        proj = dot(x[rows, :], wq[m], NN) + pk[m, 1:2, 0:576]
        cosine, sine = rotary(meta, tab, m, rows, ROWS)
        lane = lanes((ROWS, 128))
        even = lane < HEAD_DIM
        odd = jnp.logical_not(even)
        s = meta[rows, 2:3]
        r1 = pltpu.roll(proj[:, 128:256], HEAD_DIM, 1)
        r2 = pltpu.roll(proj[:, 256:384], HEAD_DIM, 1)
        rv = pltpu.roll(proj[:, 384:512], HEAD_DIM, 1)
        v_last = jnp.concatenate([jnp.ones((ROWS, HEAD_DIM), F32), proj[:, 512:576]], axis=1)
        qs = [proj[:, 0:128], proj[:, 128:256]]
        ks = [jnp.where(even, r1, r2), r2]
        for pair in range(2):
            sl = slice(128 * pair, 128 * pair + 128)
            c, sg = cosine[:, sl], sine[:, sl]
            qr = (qs[pair] * c + swap_halves(qs[pair]) * sg) * (HEAD_DIM**-0.5)
            kr = ks[pair] * c + swap_halves(ks[pair]) * sg
            for h in (0, 1) if pair == 0 else (2,):
                inside = even if h % 2 == 0 else odd
                j = lane - (HEAD_DIM if h % 2 == 0 else 0)
                fq = jnp.where((j < 3) & (j != s), -BIG, 0.0)
                fk = jnp.where((j == s) | ((j >= 3) & (j < 6)), 1.0, 0.0)
                qa[slot, h, rows, :] = jnp.where(inside, qr, fq).astype(BF16)
                ka[slot, h, rows, :] = jnp.where(inside, kr, fk).astype(BF16)
        va[slot, 0, rows, :] = jnp.where(even, 1.0, rv).astype(BF16)
        va[slot, 1, rows, :] = jnp.where(even, rv, 1.0).astype(BF16)
        va[slot, 2, rows, :] = v_last.astype(BF16)

    def attend(m, slot, i):
        rows = pl.ds(i * ROWS, ROWS)
        lane = lanes((ROWS, 128))
        outs = []
        for h in range(3):
            q = qa[slot, h, rows, :]
            s = dot(q, ka[slot, h], NT)
            peak = jnp.max(s, axis=1, keepdims=True)
            p = jnp.exp(s - peak).astype(BF16)
            o = dot(p, va[slot, h], NN)
            spot = 0 if h % 2 == 0 else HEAD_DIM
            base = HEAD_DIM if h % 2 == 0 else 0
            outs.append(o / pltpu.roll(o, HEAD_DIM, 1))
            high, mid, low = split3(-(peak + jnp.log(o[:, spot : spot + 1])))
            qn_ = q.astype(F32)
            qn_ = jnp.where(lane == base + 3, high.astype(F32), qn_)
            qn_ = jnp.where(lane == base + 4, mid.astype(F32), qn_)
            qn_ = jnp.where(lane == base + 5, low.astype(F32), qn_)
            qa[slot, h, rows, :] = qn_.astype(BF16)
        even = lane < HEAD_DIM
        mixed[m, rows, 0:128] = jnp.where(even, 0.0, outs[0]).astype(BF16)
        mixed[m, rows, 128:256] = jnp.where(even, outs[1], outs[2]).astype(BF16)

    plan = {
        ("a", 0, 1): [(q1, 1), (qn[2], 1), (qn[3], 1), (q1, 2)],
        ("p", 1, 0): [(ud[1], 0), (oc, 0)],
        ("p", 1, 1): [(qn[2], 2), (ud[2], 0), (ud[3], 0)],
        ("a", 1, 0): [(qn[2], 3), (qn[3], 2)],
        ("a", 1, 1): [(qn[2], 4), (qn[3], 3)],
        ("p", 2, 1): [(oc, 1), (qn[3], 4), (ud[1], 1)],
        ("a", 2, 0): [(oc, 2)],
        ("a", 2, 1): [(oc, 3), (ud[1], 2), (ud[2], 1)],
        ("p", 3, 1): [(oc, 4)],
        ("a", 3, 0): [(ud[1], 3), (ud[2], 2)],
        ("a", 3, 1): [(ud[1], 4), (ud[3], 1)],
        ("h", 0, 1): [(ud[2], 3)],
        ("u", 0, 0): [(ud[2], 4), (ud[3], 2)],
        ("u", 0, 1): [(ud[3], 3)],
        ("u", 1, 0): [(ud[3], 4)],
    }

    def pump(*key):
        for what, k in plan.get(key, ()):
            what.stage(k)

    loads[0].wait()
    for m in range(groups):
        slot = m % 2
        if m == 1:
            for n in range(1, groups):
                mail.arrive(pack_numbers[n - 1], pk.at[n], me.z[n])
                make_table(n)
            loads[2].wait()
        if m >= 2:
            for c in saves(m - 2, slot):
                c.wait()
        for i in range(steps):
            project(m, slot, i)
            pump("p", m, i)
        for i in range(steps):
            attend(m, slot, i)
            pump("a", m, i)
        for c in saves(m, slot):
            c.start()
    kept = [pltpu.make_async_copy(wq, wq_out, o_sem.at[3]), pltpu.make_async_copy(tab, tab_out, o_sem.at[4])]
    for c in kept:
        c.start()
    for c in loads[1:2] + loads[3:]:
        c.wait()

    for i in range(steps):
        rows = pl.ds(i * ROWS, ROWS)
        head_sum = dot(mixed[0, rows, :], wo[0], NN)
        for m in range(1, groups):
            head_sum += dot(mixed[m, rows, :], wo[m], NN)
        h = tok[rows, :].astype(F32) + head_sum + ob[...]
        hidden[rows, :] = h
        scaled, _ = norm_rows(h)
        x2[rows, :] = (scaled * gain2[...] + shift2[...]).astype(BF16)
        live = (meta[rows, 3:4]).astype(F32)
        cot[rows, :] = (cot[rows, :].astype(F32) * live).astype(BF16)
        pump("h", 0, i)
    sums[...] = jnp.zeros_like(sums)
    for m in range(groups):
        for i in range(steps):
            rows = pl.ds(i * ROWS, ROWS)
            xr = x2[rows, :]
            gr = cot[rows, :]
            upward = dot(xr, wud[m, 0], NN) + pk[m, 0:1, :]
            grad_activ = dot(gr, wud[m, 1], NT)
            phi, density = gelu_parts(upward)
            activ = (upward * phi).astype(BF16)
            grad_up = (grad_activ * (phi + upward * density)).astype(BF16)
            unit = dot(activ, wud[m, 1], NN)
            grad_in = dot(grad_up, wud[m, 0], NT)
            if m == 0:
                unit_acc[rows, :] = unit
                grad_acc[rows, :] = grad_in
                down, up = dot(activ, gr, TN), dot(xr, grad_up, TN)
                if i == 0:
                    dwd[...] = down
                    dwu[...] = up
                else:
                    dwd[...] += down
                    dwu[...] += up
                sums[4:5, :] += jnp.sum(grad_up.astype(F32), axis=0, keepdims=True)
            else:
                unit_acc[rows, :] += unit
                grad_acc[rows, :] += grad_in
            pump("u", m, i)
    x_store.wait()
    for i in range(steps):
        rows = pl.ds(i * ROWS, ROWS)
        h = hidden[rows, :]
        live = (meta[rows, 3:4]).astype(F32)
        out[rows, :] = (live * (h + unit_acc[rows, :] + db[...])).astype(BF16)
        scaled, inverse = norm_rows(h)
        grad_result = cot[rows, :].astype(F32)
        grad_x = grad_acc[rows, :]
        grad_hidden = grad_result + norm_back(grad_x, scaled, inverse, gain2[...])
        hidden[rows, :] = grad_hidden
        low = grad_hidden.astype(BF16)
        sums[0:1, :] += jnp.sum(grad_x * scaled, axis=0, keepdims=True)
        sums[1:2, :] += jnp.sum(grad_x, axis=0, keepdims=True)
        sums[2:3, :] += jnp.sum(grad_hidden, axis=0, keepdims=True)
        sums[3:4, :] += jnp.sum(grad_result, axis=0, keepdims=True)
        part = dot(mixed[0, rows, :], low, TN)
        if i == 0:
            dwo[...] = part
        else:
            dwo[...] += part
        lane = lanes((ROWS, 128))
        even = lane < HEAD_DIM
        for m in range(groups):
            grad_mixed = dot(low, wo[m], NT).astype(BF16).astype(F32)
            for head in range(3):
                sl = slice(0, 128) if head == 0 else slice(128, 256)
                product = grad_mixed[:, sl] * mixed[m, rows, sl].astype(F32)
                inside = even if head % 2 == 1 else jnp.logical_not(even)
                base = 0 if head % 2 == 0 else HEAD_DIM
                inner = jnp.sum(jnp.where(inside, product, 0.0), axis=1, keepdims=True)
                high, mid, lo = split3(-inner)
                value = jnp.where(inside, grad_mixed[:, sl], 0.0)
                value = jnp.where(lane == base, high.astype(F32), value)
                value = jnp.where(lane == base + 1, mid.astype(F32), value)
                value = jnp.where(lane == base + 2, lo.astype(F32), value)
                dos[m, head, rows, :] = value.astype(BF16)
    last = [
        pltpu.make_async_copy(dos, do_out, o_sem.at[0]),
        pltpu.make_async_copy(out, out_out, o_sem.at[1]),
        pltpu.make_async_copy(hidden, gh_out, o_sem.at[2]),
    ]
    for c in last:
        c.start()
    for m in range(max(groups - 2, 0), groups):
        for c in saves(m, m % 2):
            c.wait()
    for c in last + kept:
        c.wait()
    mail.finish()


def front(groups, tok, posr, counts, gain1, shift1, pack, ob, gain2, shift2, db, cot, wq, wo, wu, wd):
    total, width = tok.shape
    units = wu.shape[1]
    sds = jax.ShapeDtypeStruct
    heads = sds((groups, 3, total, 128), BF16)
    outs = [heads] * 4 + [
        sds((total, width), BF16), sds((total, width), F32), sds((total, width), BF16),
        sds((groups,) + wq.shape, BF16), sds((groups, 2, 128, 512), BF16), sds((total, 8), jnp.int32),
        sds((256, width), F32), sds((width, units), F32), sds((units, width), F32), sds((8, width), F32),
    ]
    slot = pltpu.VMEM((2, 3, total, 128), BF16)
    rowsb = pltpu.VMEM((total, width), BF16)
    rowsf = pltpu.VMEM((total, width), F32)
    return pl.pallas_call(
        functools.partial(front_body, groups),
        out_shape=outs,
        in_specs=[VMEM] * 2 + [SMEM] + [VMEM] * 7 + [ANY] * 5,
        out_specs=[ANY] * 9 + [VMEM] * 5,
        scratch_shapes=[
            pltpu.VMEM((groups,) + wq.shape, BF16), pltpu.VMEM((groups, 256, width), BF16),
            pltpu.VMEM((groups, 2, width, units), BF16), pltpu.VMEM((groups, 8, width), F32),
            pltpu.VMEM((groups, 2, 128, 512), BF16), pltpu.VMEM((8, total), F32),
            rowsb, rowsb, slot, slot, slot,
            pltpu.VMEM((groups, total, 256), BF16), rowsf, rowsb, rowsf, rowsf,
            pltpu.VMEM((groups, 3, total, 128), BF16), rowsb,
            pltpu.SemaphoreType.DMA((5,)), pltpu.SemaphoreType.DMA((2, 4)), pltpu.SemaphoreType.DMA((5,)),
            pltpu.SemaphoreType.DMA((FRONT_MESSAGES,)), pltpu.SemaphoreType.DMA((FRONT_MESSAGES,)),
        ],
        compiler_params=pltpu.CompilerParams(
            vmem_limit_bytes=62 * 1024 * 1024, collective_id=0, has_side_effects=True
        ),
        name="front",
    )(tok, posr, counts, gain1, shift1, pack, ob, gain2, shift2, db, cot, wq, wo, wu, wd)


def back_body(
    groups, tok, meta, gain1, tab, qa_in, ka_in, va_in, do_in, x_in, gh_in, wq_in,
    gtok, dw, small, sums,
    qa, ka, va, do, wq, x, gh, gx, kt, dqt, dk, dv, l_sem, c_sem,
):
    total = tok.shape[0]
    steps = total // ROWS

    def loads(m):
        slot = m % 2
        pairs = ((qa_in, qa), (ka_in, ka), (va_in, va), (do_in, do), (wq_in, wq))
        return [pltpu.make_async_copy(a.at[m], b.at[slot], l_sem.at[slot, n]) for n, (a, b) in enumerate(pairs)]

    extra = [pltpu.make_async_copy(x_in, x, c_sem.at[0]), pltpu.make_async_copy(gh_in, gh, c_sem.at[1])]
    for c in loads(0):
        c.start()
    for c in extra:
        c.start()
    dw[...] = jnp.zeros_like(dw)
    small[...] = jnp.zeros_like(small)
    sums[...] = jnp.zeros_like(sums)
    for m in range(groups):
        slot = m % 2
        if m + 1 < groups:
            for c in loads(m + 1):
                c.start()
        for c in loads(m):
            c.wait()
        dqt[...] = jnp.zeros_like(dqt)
        for h in range(3):
            base = 0 if h % 2 == 0 else HEAD_DIM
            flipped = jnp.transpose(ka[slot, h].astype(F32))
            kt[HEAD_DIM * h : HEAD_DIM * h + HEAD_DIM, :] = flipped[base : base + HEAD_DIM, :].astype(BF16)

        def block(i, carry, slot=slot):
            keys = pl.ds(pl.multiple_of(i * KEYS, KEYS), KEYS)
            dks, dvs = [], []
            for h in range(3):
                q = qa[slot, h]
                g = do[slot, h]
                p = jnp.exp(dot(ka[slot, h, keys, :], q, NT))
                dp = dot(va[slot, h, keys, :], g, NT)
                ds = (p * dp).astype(BF16)
                dvs.append(dot(p.astype(BF16), g, NN))
                dks.append(dot(ds, q, NN))
                mine = slice(HEAD_DIM * h, HEAD_DIM * h + HEAD_DIM)
                dqt[mine, :] += dot(kt[mine, keys], ds, NN)
            even = even_lanes((KEYS, 128))
            dk[keys, 0:128] = jnp.where(even, dks[0], dks[1])
            dk[keys, 128:256] = jnp.where(even, dks[2], 0.0)
            turned = [pltpu.roll(v, HEAD_DIM, 1) for v in dvs]
            dv[keys, 0:128] = jnp.where(even, turned[0], turned[1]).astype(BF16)
            dv[keys, 128:256] = turned[2].astype(BF16)
            return carry

        lax.fori_loop(0, total // KEYS, block, 0)
        if m == 0:
            for c in extra:
                c.wait()

        def finish(i, carry, m=m, slot=slot):
            rows = row_block(i)
            cosine, sine = rotary(meta, tab, m, rows, ROWS)
            even = even_lanes((ROWS, 128))
            dq = jnp.transpose(dqt[:, rows]) * (HEAD_DIM**-0.5)
            grads = [[dq[:, :128], dq[:, 128:]], [dk[rows, :128], dk[rows, 128:]]]
            plain = [
                [g[p] * cosine[:, 128 * p : 128 * p + 128] - swap_halves(g[p]) * sine[:, 128 * p : 128 * p + 128] for p in range(2)]
                for g in grads
            ]
            r0 = pltpu.roll(plain[1][0], HEAD_DIM, 1)
            r1 = pltpu.roll(plain[1][1], HEAD_DIM, 1)
            flat = jnp.concatenate(
                [
                    plain[0][0].astype(BF16),
                    jnp.where(even, plain[0][1], r0).astype(BF16),
                    jnp.where(even, r0, r1).astype(BF16),
                    dv[rows, :192],
                ],
                axis=1,
            )
            acc = dot(flat, wq[slot], NT)
            if m == 0:
                zero = jnp.zeros((ROWS, 128), F32)
                angle = []
                for p in range(2):
                    odd_q = qa[slot, 1, rows, :].astype(F32) if p == 0 else zero
                    odd_k = ka[slot, 1, rows, :].astype(F32) if p == 0 else zero
                    q = jnp.where(even, qa[slot, 2 * p, rows, :].astype(F32), odd_q) * (HEAD_DIM**0.5)
                    k = jnp.where(even, ka[slot, 2 * p, rows, :].astype(F32), odd_k)
                    term = grads[0][p] * swap_halves(q) + grads[1][p] * swap_halves(k)
                    first = lanes(term.shape) % HEAD_DIM < HALF
                    angle.append(jnp.where(first, -term, term))
                angle = jnp.concatenate(angle, axis=1)
                for axis in range(2):
                    p = meta[rows, axis : axis + 1].astype(F32)
                    small[axis : axis + 1, 0:256] += jnp.sum(angle * p, axis=0, keepdims=True)
                small[2:3, 0:576] += jnp.sum(flat.astype(F32), axis=0, keepdims=True)
                dw[...] += dot(x[rows, :], flat, TN)
            if m > 0:
                acc += gx[rows, :]
            if m == groups - 1:
                scaled, inverse = norm_rows(tok[rows, :].astype(F32))
                sums[0:1, :] += jnp.sum(acc * scaled, axis=0, keepdims=True)
                sums[1:2, :] += jnp.sum(acc, axis=0, keepdims=True)
                gtok[rows, :] = (gh[rows, :] + norm_back(acc, scaled, inverse, gain1[...])).astype(BF16)
            else:
                gx[rows, :] = acc
            return carry

        lax.fori_loop(0, steps, finish, 0)


def back(groups, tok, meta, gain1, tab, qa, ka, va, do, x, gh, wq):
    total, width = tok.shape
    sds = jax.ShapeDtypeStruct
    slot = pltpu.VMEM((2, 3, total, 128), BF16)
    return pl.pallas_call(
        functools.partial(back_body, groups),
        out_shape=[
            sds((total, width), BF16), sds((width, 576), F32), sds((8, 640), F32), sds((8, width), F32),
        ],
        in_specs=[VMEM] * 4 + [ANY] * 7,
        out_specs=[VMEM] * 4,
        scratch_shapes=[
            slot, slot, slot, slot, pltpu.VMEM((2,) + wq.shape[1:], BF16), pltpu.VMEM((total, width), BF16),
            pltpu.VMEM((total, width), F32), pltpu.VMEM((total, width), F32),
            pltpu.VMEM((256, total), BF16), pltpu.VMEM((256, total), F32),
            pltpu.VMEM((total, 256), F32), pltpu.VMEM((total, 256), BF16),
            pltpu.SemaphoreType.DMA((2, 5)), pltpu.SemaphoreType.DMA((2,)),
        ],
        compiler_params=PARAMS,
        name="back",
    )(tok, meta, gain1, tab, qa, ka, va, do, x, gh, wq)


def body(
    n_tensor, tokens, cotangent, kept_counts, patch_pos, attn_gain, attn_shift, qkv_weight, qkv_bias,
    rope_freq, out_weight, out_bias, mlp_gain, mlp_shift, up_weight, up_bias, down_weight, down_bias,
):
    total, width = tokens.shape
    cols = qkv_weight.shape[2]
    heads = cols // HEAD_DIM
    groups = n_tensor
    row = lambda v: v.reshape(1, -1)
    freq = jnp.broadcast_to(rope_freq.reshape(2, heads, 1, HALF), (2, heads, 2, HALF)).reshape(2, cols)
    wide = lambda v: jnp.pad(v, ((0, 0), (0, width - v.shape[1])))
    pack = jnp.concatenate(
        [row(up_bias), wide(qkv_bias.reshape(1, 3 * cols)), wide(freq), jnp.zeros((4, width), F32)]
    )
    wq = qkv_weight.reshape(width, 3 * cols)
    qa, ka, va, do, block_out, gh, x, wq_all, tab, meta, dwo, dwu, dwd, sums = front(
        groups, tokens, patch_pos, kept_counts, row(attn_gain), row(attn_shift), pack, row(out_bias),
        row(mlp_gain), row(mlp_shift), row(down_bias), cotangent, wq, out_weight, up_weight, down_weight,
    )
    grad_tokens, dw, small, first_sums = back(
        groups, tokens, meta, row(attn_gain), tab, qa, ka, va, do, x, gh, wq_all
    )
    grad_qkv = dw.reshape(width, 3, cols)
    grad_qkv_bias = small[2, : 3 * cols].reshape(3, cols)
    angles = small[0:2, :cols].reshape(2, heads, 2, HALF)
    grad_freq = (angles[:, :, 0] + angles[:, :, 1]).reshape(2, heads * HALF)
    outs = (
        first_sums[0], first_sums[1], grad_qkv, grad_qkv_bias, grad_freq, dwo[256 - cols :], sums[2], sums[0],
        sums[1], dwu, sums[4], dwd, sums[3],
    )
    outs = lax.psum(outs, "dp")
    return (block_out, grad_tokens) + tuple(outs)


def solution(mesh):
    return jax.shard_map(
        functools.partial(body, mesh.shape["tensor"]),
        mesh=mesh,
        in_specs=(
            P("dp", None), P("dp", None), P("dp"), P(None, "dp"), P(), P(), P(None, None, "tensor"),
            P(None, "tensor"), P(None, "tensor"), P("tensor", None), P(), P(), P(), P(None, "tensor"),
            P("tensor"), P("tensor", None), P(),
        ),
        out_specs=(
            P("dp", None), P("dp", None), P(), P(), P(None, None, "tensor"), P(None, "tensor"),
            P(None, "tensor"), P("tensor", None), P(), P(), P(), P(None, "tensor"), P("tensor"),
            P("tensor", None), P(),
        ),
        check_vma=False,
    )
```

```python
import functools

import jax
import jax.numpy as jnp
from jax import lax
from jax.experimental import pallas as pl
from jax.experimental.pallas import tpu as pltpu
from jax.sharding import PartitionSpec as P

HEAD_DIM = 64
HALF = HEAD_DIM // 2
GRID_SIDE = 24
EPS = 1e-06
BIG = 1e30
F32 = jnp.float32
BF16 = jnp.bfloat16
NN = (((1,), (0,)), ((), ()))
NT = (((1,), (1,)), ((), ()))
TN = (((0,), (0,)), ((), ()))
VMEM = pl.BlockSpec(memory_space=pltpu.VMEM)
SMEM = pl.BlockSpec(memory_space=pltpu.SMEM)
ANY = pl.BlockSpec(memory_space=pl.ANY)
MESH = pl.DeviceIdType.MESH
TABLE_ROWS = 32
PEERS = 8
PARAMS = pltpu.CompilerParams(vmem_limit_bytes=60 * 1024 * 1024)


def dot(a, b, dims):
    return lax.dot_general(a, b, dims, preferred_element_type=F32)


def lanes(shape):
    return lax.broadcasted_iota(jnp.int32, shape, len(shape) - 1)


def norm_rows(values):
    center = values - jnp.mean(values, axis=-1, keepdims=True)
    inverse = lax.rsqrt(jnp.mean(center * center, axis=-1, keepdims=True) + EPS)
    return center * inverse, inverse


def norm_back(grad_out, scaled, inverse, gain):
    grad_scaled = grad_out * gain
    inner = jnp.mean(grad_scaled, axis=-1, keepdims=True)
    along = jnp.mean(grad_scaled * scaled, axis=-1, keepdims=True)
    return inverse * (grad_scaled - inner - scaled * along)


def swap_halves(u):
    first = lanes(u.shape) % HEAD_DIM < HALF
    return jnp.where(first, pltpu.roll(u, 128 - HALF, 1), pltpu.roll(u, HALF, 1))


def split3(v):
    high = v.astype(BF16)
    rest = v - high.astype(F32)
    mid = rest.astype(BF16)
    low = (rest - mid.astype(F32)).astype(BF16)
    return high, mid, low


def gelu_parts(v):
    x = jnp.abs(v) * 0.7071067811865476
    t = 1.0 / (1.0 + 0.3275911 * x)
    e = jnp.exp(-(x * x))
    poly = t * (
        0.254829592
        + t * (-0.284496736 + t * (1.421413741 + t * (-1.453152027 + t * 1.061405429)))
    )
    tail = 0.5 * poly * e
    phi = jnp.where(v >= 0, 1.0 - tail, tail)
    return phi, e * 0.3989422804014327


ROWS = 512
KEYS = 256


def even_lanes(shape):
    return lanes(shape) < HEAD_DIM


def rotary(meta, tab, m, rows, count):
    lane = lanes((count, 128))
    parts = []
    for axis in range(2):
        p = meta[rows, axis : axis + 1]
        hot = (lane == p) | (lane == p + TABLE_ROWS) | (lane == p + 2 * TABLE_ROWS)
        parts.append(dot(hot.astype(F32).astype(BF16), tab[m, axis], NN))
    rc, rs = parts[0][:, :256], parts[0][:, 256:]
    cc, sc = parts[1][:, :256], parts[1][:, 256:]
    cosine = rc * cc - rs * sc
    sine = rs * cc + rc * sc
    sine = jnp.where(lanes(sine.shape) % HEAD_DIM < HALF, -sine, sine)
    return cosine, sine


def as_row(ref):
    return ref[...].reshape(1, ref.shape[0])


def row_block(i):
    return pl.ds(pl.multiple_of(i * ROWS, ROWS), ROWS)


class Places:
    def __init__(self):
        d, t = lax.axis_index("dp"), lax.axis_index("tensor")
        self.d, self.t = d, t
        low = d % PEERS
        b0, b1, b2 = low % 2, (low // 2) % 2, low // 4
        core, across_x, across_y = 1 - 2 * b0, 2 - 4 * b1, 4 - 8 * b2
        t0, t1 = t % 2, (t // 2) % 2
        flip0, flip1 = 1 - 2 * t0, 2 - 4 * t1
        self.slice = low
        self.slice_x, self.slice_y = low + across_x, low + across_y
        self.slice_xy = low + across_x + across_y
        self.core_step = core
        self.half = b0
        self.core = (d + core, t)
        self.x = (d + across_x, t)
        self.y = (d + across_y, t)
        self.xy = (d + across_x + across_y, t)
        j, jx, jy = b1 + 2 * b2, 1 - 2 * b1, 2 - 4 * b2
        self.quarter, self.quarter_x, self.quarter_y, self.quarter_xy = j, j + jx, j + jy, j + jx + jy
        self.far = []
        step = PEERS
        while step < lax.axis_size("dp"):
            self.far.append((d + step - 2 * step * ((d // step) % 2), t))
            step *= 2
        self.z = [None, (d, t + flip0), (d, t + flip1), (d, t + flip0 + flip1)]


def greet(partners):
    barrier = pltpu.get_barrier_semaphore()
    for p in partners:
        pl.semaphore_signal(barrier, inc=1, device_id=p, device_id_type=MESH)
    pl.semaphore_wait(barrier, len(partners))


class Mail:
    def __init__(self, send_sem, recv_sem):
        self.send_sem, self.recv_sem = send_sem, recv_sem
        self.count = 0
        self.sent = []

    def number(self):
        self.count += 1
        return self.count - 1

    def send(self, n, src, dst, device):
        copy = pltpu.make_async_remote_copy(
            src_ref=src, dst_ref=dst, send_sem=self.send_sem.at[n], recv_sem=self.recv_sem.at[n],
            device_id=device, device_id_type=MESH,
        )
        copy.start()
        self.sent.append(copy)

    def arrive(self, n, dst, device):
        pltpu.make_async_remote_copy(
            src_ref=dst, dst_ref=dst, send_sem=self.send_sem.at[n], recv_sem=self.recv_sem.at[n],
            device_id=device, device_id_type=MESH,
        ).wait_recv()

    def finish(self):
        for copy in self.sent:
            copy.wait_send()


class Sliced:
    def __init__(self, mail, me, sources, targets, view, height):
        self.mail, self.me, self.view, self.height = mail, me, view, height
        self.transfers = targets
        self.z = [mail.number() for _ in targets]
        self.n = [mail.number() for _ in range(8)]

    def piece(self, s, off=0, size=None):
        size = self.height if size is None else size
        return self.view(pl.ds(pl.multiple_of(s * self.height + off, 16), size))

    def stage(self, k):
        mail, me, n = self.mail, self.me, self.n
        half = self.height // 2
        mine, sx, sy, sxy = me.slice, me.slice_x, me.slice_y, me.slice_xy
        if k == 0:
            for i, (device, source, landing) in zip(self.z, self.transfers):
                rows = pl.ds(pl.multiple_of(mine * self.height, 16), self.height)
                mail.send(i, source(rows), landing(rows), device)
        elif k == 1:
            for i, (device, source, landing) in zip(self.z, self.transfers):
                rows = pl.ds(pl.multiple_of(mine * self.height, 16), self.height)
                mail.arrive(i, landing(rows), device)
            mail.send(n[0], self.piece(mine), self.piece(mine), me.x)
            mail.send(n[1], self.piece(mine), self.piece(mine), me.y)
            mail.send(n[2], self.piece(mine), self.piece(mine), me.core)
        elif k == 2:
            mail.arrive(n[0], self.piece(sx), me.x)
            mail.send(n[3], self.piece(sx, 0, half), self.piece(sx, 0, half), me.y)
            mail.send(n[5], self.piece(sx), self.piece(sx), me.core)
            mail.arrive(n[1], self.piece(sy), me.y)
            mail.send(n[4], self.piece(sy, half, half), self.piece(sy, half, half), me.x)
            mail.send(n[6], self.piece(sy), self.piece(sy), me.core)
        elif k == 3:
            mail.arrive(n[3], self.piece(sxy, 0, half), me.y)
            mail.arrive(n[4], self.piece(sxy, half, half), me.x)
            mail.send(n[7], self.piece(sxy), self.piece(sxy), me.core)
        else:
            for i, s in ((2, mine), (5, sx), (6, sy), (7, sxy)):
                mail.arrive(n[i], self.piece(s + me.core_step), me.core)


class Direct:
    def __init__(self, mail, me, device, source, landing, height):
        self.mail, self.me = mail, me
        self.device, self.source, self.landing, self.height = device, source, landing, height
        self.n = [mail.number(), mail.number()]

    def stage(self, k):
        mail, me = self.mail, self.me
        mine = pl.ds(pl.multiple_of(me.half * self.height, 16), self.height)
        other = pl.ds(pl.multiple_of((1 - me.half) * self.height, 16), self.height)
        if k == 0:
            mail.send(self.n[0], self.source(mine), self.landing(mine), self.device)
        elif k == 1:
            mail.arrive(self.n[0], self.landing(mine), self.device)
            mail.send(self.n[1], self.landing(mine), self.landing(mine), me.core)
        else:
            mail.arrive(self.n[1], self.landing(other), me.core)


FRONT_MESSAGES = 80


def front_body(
    groups, tok, posr, counts, bias, freq, up_bias, gain1, shift1, ob, gain2, shift2, db,
    cot_in, wq_in, wo_in, wu_in, wd_in,
    qa_out, ka_out, va_out, do_out, out_out, gh_out, x_out, wq_out, tab_out, meta, dwo, dwu, dwd, sums,
    part_u, part_d, wq, wo, wud, pk, tab, flipped, cot, x, qa, ka, va, mixed, hidden, x2, unit_acc, grad_acc, dos, out,
    w_sem, s_sem, o_sem, send_sem, recv_sem,
):
    total = tok.shape[0]
    cols = wo_in.shape[0]
    width = tok.shape[1]
    steps = total // ROWS
    me = Places()
    mail = Mail(send_sem, recv_sem)
    lift = 256 - cols
    gain1, shift1, ob, gain2, shift2, db = (as_row(v) for v in (gain1, shift1, ob, gain2, shift2, db))
    loads = [
        pltpu.make_async_copy(wq_in, wq.at[0], w_sem.at[0]),
        pltpu.make_async_copy(cot_in, cot, w_sem.at[1]),
        pltpu.make_async_copy(wo_in, wo.at[0, pl.ds(lift, cols), :], w_sem.at[2]),
        pltpu.make_async_copy(wu_in, wud.at[0, 0], w_sem.at[3]),
        pltpu.make_async_copy(wd_in, wud.at[0, 1], w_sem.at[4]),
    ]
    for c in loads:
        c.start()
    pack_numbers = [mail.number() for _ in range(groups - 1)]
    q1 = Direct(mail, me, me.z[1], lambda r: wq_in.at[r, :], lambda r: wq.at[1, r, :], width // 2)
    qh = width // PEERS
    qn = {
        m: Sliced(
            mail, me, None, [(me.z[m], lambda r: wq_in.at[r, :], lambda r, m=m: wq.at[m, r, :])],
            lambda r, m=m: wq.at[m, r, :], qh,
        )
        for m in range(2, groups)
    }
    oc = Sliced(
        mail, me, None,
        [(me.z[m], lambda r: wo.at[0, r, :], lambda r, m=m: wo.at[m, r, :]) for m in range(1, groups)],
        lambda r: wo.at[pl.ds(1, groups - 1), r, :], 256 // PEERS,
    )
    ud = {
        m: Sliced(
            mail, me, None,
            [
                (me.z[m], lambda r: wu_in.at[r, :], lambda r, m=m: wud.at[m, 0, r, :]),
                (me.z[m], lambda r: wd_in.at[r, :], lambda r, m=m: wud.at[m, 1, r, :]),
            ],
            lambda r, m=m: wud.at[m, :, r, :], width // PEERS,
        )
        for m in range(1, groups)
    }
    wo[0, 0:lift, :] = jnp.zeros((lift, width), BF16)
    pk[0] = jnp.zeros((8, width), F32)
    pk[0, 0:1, :] = as_row(up_bias)
    pk[0, 1:2, 0 : 3 * cols] = jnp.concatenate([bias[n : n + 1, :] for n in range(3)], axis=1)
    by_lane = [freq[:, HALF * (n // 2) : HALF * (n // 2) + HALF] for n in range(2 * (cols // HEAD_DIM))]
    pk[0, 2:4, 0:cols] = jnp.concatenate(by_lane, axis=1)
    greet(me.z[1:] + [me.core, me.x, me.y])
    for m in range(1, groups):
        mail.send(pack_numbers[m - 1], pk.at[0], pk.at[m], me.z[m])
    q1.stage(0)

    flipped[...] = jnp.zeros_like(flipped)
    flipped[0:2, :] = posr[...].astype(F32)
    place = lax.broadcasted_iota(jnp.int32, (total, 8), 0)
    end = counts[0]
    segment = (place >= end).astype(jnp.int32)
    for n in range(1, counts.shape[0]):
        end = end + counts[n]
        segment += (place >= end).astype(jnp.int32)
    alive = (place < end).astype(jnp.int32)
    lane8 = lanes((total, 8))
    meta[...] = jnp.where(
        lane8 == 2, segment, jnp.where(lane8 == 3, alive, jnp.transpose(flipped[...]).astype(jnp.int32))
    )

    def make_table(m):
        place = lax.broadcasted_iota(jnp.int32, (TABLE_ROWS, 256), 0).astype(F32)
        for axis in range(2):
            angle = place * pk[m, 2 + axis : 3 + axis, 0:256]
            for n, part in enumerate(split3(jnp.concatenate([jnp.cos(angle), jnp.sin(angle)], axis=1))):
                tab[m, axis, TABLE_ROWS * n : TABLE_ROWS * (n + 1), :] = part
            tab[m, axis, 3 * TABLE_ROWS :, :] = jnp.zeros((128 - 3 * TABLE_ROWS, 512), BF16)

    plan = {
("n", 0, 1): [(qn[2], 0), (qn[3], 0)],
        ("p", 1, 1): [(qn[2], 2)],
        ("a", 1, 0): [(qn[2], 3), (qn[3], 2)],
        ("a", 2, 0): [(oc, 2)],
        ("a", 0, 1): [(q1, 1), (qn[2], 1), (qn[3], 1), (ud[1], 0), (oc, 0), (ud[2], 0), (q1, 2)],
        ("a", 1, 1): [(ud[3], 0), (qn[3], 3), (qn[2], 4)],
        ("p", 2, 1): [(oc, 1), (qn[3], 4)],
        ("a", 2, 1): [(oc, 3), (ud[1], 1)],
        ("p", 3, 1): [(oc, 4)],
        ("a", 3, 1): [(ud[1], 2), (ud[2], 1)],
        ("h", 0, 1): [(ud[1], 3)],
        ("u", 0, 0): [(ud[2], 2), (ud[3], 1)],
        ("u", 0, 1): [(ud[1], 4), (ud[2], 3)],
        ("u", 1, 0): [(ud[3], 2)],
        ("u", 1, 1): [(ud[2], 4), (ud[3], 3)],
        ("u", 2, 1): [(ud[3], 4)],
    }

    def pump(*key):
        for what, k in plan.get(key, ()):
            what.stage(k)

    make_table(0)
    for i in range(steps):
        rows = pl.ds(i * ROWS, ROWS)
        scaled, _ = norm_rows(tok[rows, :].astype(F32))
        x[rows, :] = (scaled * gain1 + shift1).astype(BF16)
        pump("n", 0, i)
    x_store = pltpu.make_async_copy(x, x_out, s_sem.at[0, 3])
    x_store.start()

    def saves(m, slot):
        return [
            pltpu.make_async_copy(a.at[slot], b.at[m], s_sem.at[slot, n])
            for n, (a, b) in enumerate(((qa, qa_out), (ka, ka_out), (va, va_out)))
        ]

    def project(m, slot, i):
        rows = pl.ds(i * ROWS, ROWS)
        proj = dot(x[rows, :], wq[m], NN) + pk[m, 1:2, 0:576]
        cosine, sine = rotary(meta, tab, m, rows, ROWS)
        lane = lanes((ROWS, 128))
        even = lane < HEAD_DIM
        odd = jnp.logical_not(even)
        s = meta[rows, 2:3]
        r1 = pltpu.roll(proj[:, 128:256], HEAD_DIM, 1)
        r2 = pltpu.roll(proj[:, 256:384], HEAD_DIM, 1)
        rv = pltpu.roll(proj[:, 384:512], HEAD_DIM, 1)
        v_last = jnp.concatenate([jnp.ones((ROWS, HEAD_DIM), F32), proj[:, 512:576]], axis=1)
        qs = [proj[:, 0:128], proj[:, 128:256]]
        ks = [jnp.where(even, r1, r2), r2]
        for pair in range(2):
            sl = slice(128 * pair, 128 * pair + 128)
            c, sg = cosine[:, sl], sine[:, sl]
            qr = (qs[pair] * c + swap_halves(qs[pair]) * sg) * (HEAD_DIM**-0.5)
            kr = ks[pair] * c + swap_halves(ks[pair]) * sg
            for h in (0, 1) if pair == 0 else (2,):
                inside = even if h % 2 == 0 else odd
                j = lane - (HEAD_DIM if h % 2 == 0 else 0)
                fq = jnp.where((j < 3) & (j != s), -BIG, 0.0)
                fk = jnp.where((j == s) | ((j >= 3) & (j < 6)), 1.0, 0.0)
                qa[slot, h, rows, :] = jnp.where(inside, qr, fq).astype(BF16)
                ka[slot, h, rows, :] = jnp.where(inside, kr, fk).astype(BF16)
        va[slot, 0, rows, :] = jnp.where(even, 1.0, rv).astype(BF16)
        va[slot, 1, rows, :] = jnp.where(even, rv, 1.0).astype(BF16)
        va[slot, 2, rows, :] = v_last.astype(BF16)

    def attend(m, slot, i):
        rows = pl.ds(i * ROWS, ROWS)
        lane = lanes((ROWS, 128))
        outs = []
        for h in range(3):
            q = qa[slot, h, rows, :]
            s = dot(q, ka[slot, h], NT)
            peak = jnp.max(s, axis=1, keepdims=True)
            p = jnp.exp(s - peak).astype(BF16)
            o = dot(p, va[slot, h], NN)
            spot = 0 if h % 2 == 0 else HEAD_DIM
            base = HEAD_DIM if h % 2 == 0 else 0
            outs.append(o / pltpu.roll(o, HEAD_DIM, 1))
            high, mid, low = split3(-(peak + jnp.log(o[:, spot : spot + 1])))
            qn_ = q.astype(F32)
            qn_ = jnp.where(lane == base + 3, high.astype(F32), qn_)
            qn_ = jnp.where(lane == base + 4, mid.astype(F32), qn_)
            qn_ = jnp.where(lane == base + 5, low.astype(F32), qn_)
            qa[slot, h, rows, :] = qn_.astype(BF16)
        even = lane < HEAD_DIM
        mixed[m, rows, 0:128] = jnp.where(even, 0.0, outs[0]).astype(BF16)
        mixed[m, rows, 128:256] = jnp.where(even, outs[1], outs[2]).astype(BF16)

    loads[0].wait()
    loads[2].wait()
    for m in range(groups):
        slot = m % 2
        if m == 1:
            for n in range(1, groups):
                mail.arrive(pack_numbers[n - 1], pk.at[n], me.z[n])
                make_table(n)
        if m >= 2:
            for c in saves(m - 2, slot):
                c.wait()
        for i in range(steps):
            project(m, slot, i)
            pump("p", m, i)
        for i in range(steps):
            attend(m, slot, i)
            pump("a", m, i)
        for c in saves(m, slot):
            c.start()
    kept = [pltpu.make_async_copy(wq, wq_out, o_sem.at[3]), pltpu.make_async_copy(tab, tab_out, o_sem.at[4])]
    for c in kept:
        c.start()
    for c in loads[1:2] + loads[3:]:
        c.wait()

    for i in range(steps):
        rows = pl.ds(i * ROWS, ROWS)
        head_sum = dot(mixed[0, rows, :], wo[0], NN)
        for m in range(1, groups):
            head_sum += dot(mixed[m, rows, :], wo[m], NN)
        h = tok[rows, :].astype(F32) + head_sum + ob
        hidden[rows, :] = h
        scaled, _ = norm_rows(h)
        x2[rows, :] = (scaled * gain2 + shift2).astype(BF16)
        live = (meta[rows, 3:4]).astype(F32)
        cot[rows, :] = (cot[rows, :].astype(F32) * live).astype(BF16)
        pump("h", 0, i)
    sums[...] = jnp.zeros_like(sums)
    for m in range(groups):
        for i in range(steps):
            rows = pl.ds(i * ROWS, ROWS)
            xr = x2[rows, :]
            gr = cot[rows, :]
            upward = dot(xr, wud[m, 0], NN) + pk[m, 0:1, :]
            grad_activ = dot(gr, wud[m, 1], NT)
            phi, density = gelu_parts(upward)
            activ = (upward * phi).astype(BF16)
            grad_up = (grad_activ * (phi + upward * density)).astype(BF16)
            unit = dot(activ, wud[m, 1], NN)
            grad_in = dot(grad_up, wud[m, 0], NT)
            if m == 0:
                unit_acc[rows, :] = unit
                grad_acc[rows, :] = grad_in
                down, up = dot(activ, gr, TN), dot(xr, grad_up, TN)
                if i > 0:
                    down, up = part_d[...] + down, part_u[...] + up
                if i < steps - 1:
                    part_d[...], part_u[...] = down, up
                else:
                    dwd[...], dwu[...] = down.astype(BF16), up.astype(BF16)
                sums[4:5, :] += jnp.sum(grad_up.astype(F32), axis=0, keepdims=True)
            else:
                unit_acc[rows, :] += unit
                grad_acc[rows, :] += grad_in
            pump("u", m, i)
    x_store.wait()
    for i in range(steps):
        rows = pl.ds(i * ROWS, ROWS)
        h = hidden[rows, :]
        live = (meta[rows, 3:4]).astype(F32)
        out[rows, :] = (live * (h + unit_acc[rows, :] + db)).astype(BF16)
        scaled, inverse = norm_rows(h)
        grad_result = cot[rows, :].astype(F32)
        grad_x = grad_acc[rows, :]
        grad_hidden = grad_result + norm_back(grad_x, scaled, inverse, gain2)
        hidden[rows, :] = grad_hidden
        low = grad_hidden.astype(BF16)
        sums[0:1, :] += jnp.sum(grad_x * scaled, axis=0, keepdims=True)
        sums[1:2, :] += jnp.sum(grad_x, axis=0, keepdims=True)
        sums[2:3, :] += jnp.sum(grad_hidden, axis=0, keepdims=True)
        sums[3:4, :] += jnp.sum(grad_result, axis=0, keepdims=True)
        part = dot(mixed[0, rows, :], low, TN)
        if i > 0:
            part += part_d[0:256, :]
        if i < steps - 1:
            part_d[0:256, :] = part
        else:
            dwo[...] = part.astype(BF16)
        lane = lanes((ROWS, 128))
        even = lane < HEAD_DIM
        for m in range(groups):
            grad_mixed = dot(low, wo[m], NT).astype(BF16).astype(F32)
            for head in range(3):
                sl = slice(0, 128) if head == 0 else slice(128, 256)
                product = grad_mixed[:, sl] * mixed[m, rows, sl].astype(F32)
                inside = even if head % 2 == 1 else jnp.logical_not(even)
                base = 0 if head % 2 == 0 else HEAD_DIM
                inner = jnp.sum(jnp.where(inside, product, 0.0), axis=1, keepdims=True)
                high, mid, lo = split3(-inner)
                value = jnp.where(inside, grad_mixed[:, sl], 0.0)
                value = jnp.where(lane == base, high.astype(F32), value)
                value = jnp.where(lane == base + 1, mid.astype(F32), value)
                value = jnp.where(lane == base + 2, lo.astype(F32), value)
                dos[m, head, rows, :] = value.astype(BF16)
    last = [
        pltpu.make_async_copy(dos, do_out, o_sem.at[0]),
        pltpu.make_async_copy(out, out_out, o_sem.at[1]),
        pltpu.make_async_copy(hidden, gh_out, o_sem.at[2]),
    ]
    for c in last:
        c.start()
    for m in range(max(groups - 2, 0), groups):
        for c in saves(m, m % 2):
            c.wait()
    for c in last + kept:
        c.wait()
    mail.finish()


def front(groups, tok, posr, counts, vectors, cot, wq, wo, wu, wd):
    total, width = tok.shape
    units = wu.shape[1]
    sds = jax.ShapeDtypeStruct
    heads = sds((groups, 3, total, 128), BF16)
    outs = [heads] * 4 + [
        sds((total, width), BF16), sds((total, width), F32), sds((total, width), BF16),
        sds((groups,) + wq.shape, BF16), sds((groups, 2, 128, 512), BF16), sds((total, 8), jnp.int32),
        sds((256, width), BF16), sds((width, units), BF16), sds((units, width), BF16), sds((8, width), F32),
    ]
    slot = pltpu.VMEM((2, 3, total, 128), BF16)
    rowsb = pltpu.VMEM((total, width), BF16)
    rowsf = pltpu.VMEM((total, width), F32)
    return pl.pallas_call(
        functools.partial(front_body, groups),
        out_shape=outs,
        in_specs=[VMEM] * 2 + [SMEM] + [VMEM] * len(vectors) + [ANY] * 5,
        out_specs=[ANY] * 9 + [VMEM] * 5,
        scratch_shapes=[
            pltpu.VMEM((width, units), F32), pltpu.VMEM((units, width), F32),
            pltpu.VMEM((groups,) + wq.shape, BF16), pltpu.VMEM((groups, 256, width), BF16),
            pltpu.VMEM((groups, 2, width, units), BF16), pltpu.VMEM((groups, 8, width), F32),
            pltpu.VMEM((groups, 2, 128, 512), BF16), pltpu.VMEM((8, total), F32),
            rowsb, rowsb, slot, slot, slot,
            pltpu.VMEM((groups, total, 256), BF16), rowsf, rowsb, rowsf, rowsf,
            pltpu.VMEM((groups, 3, total, 128), BF16), rowsb,
            pltpu.SemaphoreType.DMA((5,)), pltpu.SemaphoreType.DMA((2, 4)), pltpu.SemaphoreType.DMA((5,)),
            pltpu.SemaphoreType.DMA((FRONT_MESSAGES,)), pltpu.SemaphoreType.DMA((FRONT_MESSAGES,)),
        ],
        compiler_params=pltpu.CompilerParams(
            vmem_limit_bytes=62 * 1024 * 1024, collective_id=0, has_side_effects=True
        ),
        name="front",
    )(tok, posr, counts, *vectors, cot, wq, wo, wu, wd)


class Reduce:
    def __init__(self, mail, me, src, load_sem, came, own, parts, final, spare):
        self.mail, self.me, self.src, self.load_sem = mail, me, src, load_sem
        self.came, self.own, self.parts, self.final, self.spare = came, own, parts, final, spare
        self.half, self.quarter = own.shape[0], parts.shape[1]
        self.n = [mail.number() for _ in range(8 + len(me.far))]

    def band(self, start, size):
        return pl.ds(pl.multiple_of(start, 16), size)

    def load(self):
        mine = self.band(self.me.half * self.half, self.half)
        return pltpu.make_async_copy(self.src.at[mine, :], self.own, self.load_sem)

    def stage(self, k):
        mail, me, n = self.mail, self.me, self.n
        half, quarter = self.half, self.quarter
        places = ((me.x, me.quarter_x), (me.y, me.quarter_y), (me.xy, me.quarter_xy))
        spot = lambda j: self.final.at[self.band(me.half * half + j * quarter, quarter), :]
        if k == 0:
            self.load().start()
            other = self.band((1 - me.half) * half, half)
            mail.send(n[0], self.src.at[other, :], self.came, me.core)
        elif k == 1:
            self.load().wait()
            mail.arrive(n[0], self.came, me.core)
            self.own[...] = (self.own[...].astype(F32) + self.came[...].astype(F32)).astype(BF16)
            for i, (device, j) in enumerate(places):
                mail.send(n[1 + i], self.own.at[self.band(j * quarter, quarter), :], self.parts.at[i], device)
        elif k == 2:
            for i, (device, _) in enumerate(places):
                mail.arrive(n[1 + i], self.parts.at[i], device)
            total = self.own[self.band(me.quarter * quarter, quarter), :].astype(F32)
            for i in range(3):
                total += self.parts[i].astype(F32)
            for i, device in enumerate(me.far):
                self.spare[2 * i] = total.astype(BF16)
                mail.send(n[8 + i], self.spare.at[2 * i], self.spare.at[2 * i + 1], device)
                mail.arrive(n[8 + i], self.spare.at[2 * i + 1], device)
                total += self.spare[2 * i + 1].astype(F32)
            self.final[self.band(me.half * half + me.quarter * quarter, quarter), :] = total.astype(BF16)
            for i, (device, _) in enumerate(places):
                mail.send(n[4 + i], spot(me.quarter), spot(me.quarter), device)
        elif k == 3:
            for i, (device, j) in enumerate(places):
                mail.arrive(n[4 + i], spot(j), device)
            mine = self.final.at[self.band(me.half * half, half), :]
            mail.send(n[7], mine, mine, me.core)
        else:
            mail.arrive(n[7], self.final.at[self.band((1 - me.half) * half, half), :], me.core)


class ReduceSmall:
    def __init__(self, mail, me, src, hold, came):
        self.mail, self.me, self.src, self.hold, self.came = mail, me, src, hold, came
        self.n = [mail.number() for _ in range(4 + len(me.far))]

    def stage(self, k):
        mail, me, n = self.mail, self.me, self.n
        places = (me.x, me.y, me.xy)
        if k == 0:
            mail.send(n[0], self.src, self.came.at[0], me.core)
        elif k == 1:
            mail.arrive(n[0], self.came.at[0], me.core)
            self.hold[0] = self.src[...] + self.came[0]
            for i, device in enumerate(places):
                mail.send(n[1 + i], self.hold.at[0], self.came.at[1 + i], device)
        else:
            for i, device in enumerate(places):
                mail.arrive(n[1 + i], self.came.at[1 + i], device)
            total = (self.hold[0] + self.came[1]) + (self.came[2] + self.came[3])
            for i, device in enumerate(me.far):
                self.hold[1 + i] = total
                mail.send(n[4 + i], self.hold.at[1 + i], self.came.at[4 + i], device)
                mail.arrive(n[4 + i], self.came.at[4 + i], device)
                total = total + self.came[4 + i]
            return total


BACK_MESSAGES = 64


def back_body(
    groups, tok, meta, gain1, tab, front_sums, qa_in, ka_in, va_in, do_in, x_in, gh_in, wq_in, du_in, dd_in, do_w_in,
    gtok, vectors, du_out, dd_out, do_w_out, dq_out,
    dw, dwq, small, across, qa, ka, va, do, wq, x, gh, gx, kt, dqt, dk, dv,
    came_u, own_u, parts_u, final_u, came_d, own_d, parts_d, final_d, came_o, own_o, parts_o, final_o,
    came_q, own_q, parts_q, final_q, spare_u, spare_o, spare_q, hold, came_s,
    l_sem, c_sem, r_sem, send_sem, recv_sem,
):
    total = tok.shape[0]
    steps = total // ROWS
    me = Places()
    mail = Mail(send_sem, recv_sem)
    gain1 = as_row(gain1)
    cols = wq_in.shape[2] // 3
    across_numbers = [mail.number() for _ in range(groups - 1)]
    ru = Reduce(mail, me, du_in, r_sem.at[0], came_u, own_u, parts_u, final_u, spare_u.at[0])
    rd = Reduce(mail, me, dd_in, r_sem.at[1], came_d, own_d, parts_d, final_d, spare_u.at[1])
    ro = Reduce(mail, me, do_w_in, r_sem.at[2], came_o, own_o, parts_o, final_o, spare_o)
    rq = Reduce(mail, me, dwq, r_sem.at[3], came_q, own_q, parts_q, final_q, spare_q)
    small_a = ReduceSmall(mail, me, front_sums, hold.at[0], came_s.at[0])
    small_b = ReduceSmall(mail, me, small, hold.at[1], came_s.at[1])
    finals = [
        pltpu.make_async_copy(a, b, c_sem.at[2 + n])
        for n, (a, b) in enumerate(((final_u, du_out), (final_d, dd_out), (final_o.at[256 - cols :, :], do_w_out), (final_q, dq_out)))
    ]
    plan = {
        ("k", 0): [(ru, 1), (rd, 1), (ro, 1), (small_a, 1)],
        ("f", 0): [(rq, 0), (small_b, 0)],
        ("k", 1): [(small_a, 2), (rq, 1), (small_b, 1)],
        ("f", 1): [(ru, 2), (rd, 2), (ro, 2), (small_b, 2)],
        ("k", 2): [(small_b, 3)],
        ("f", 2): [(rq, 2), (ru, 3), (rd, 3), (ro, 3)],
        ("k", 3): [(ru, 4), (rd, 4), (ro, 4), (rq, 3)],
        ("f", 3): [(rq, 4)],
    }

    def pump(*key):
        for what, k in plan.get(key, ()):
            if what is small_b and k == 3:
                for n in range(1, groups):
                    mail.arrive(across_numbers[n - 1], across.at[n], me.z[n])
                total = (across[0] + across[1]) + (across[2] + across[3])
                vectors[16:24, :] = total
                continue
            value = what.stage(k)
            if what is small_a and k == 2:
                vectors[0:8, :] = value
            if what is small_b and k == 2:
                across[0] = value
                for n in range(1, groups):
                    mail.send(across_numbers[n - 1], across.at[0], across.at[n], me.z[n])
                vectors[8:16, :] = value
            for n, unit in enumerate((ru, rd, ro, rq)):
                if what is unit and k == 4:
                    finals[n].start()

    def loads(m):
        slot = m % 2
        pairs = ((qa_in, qa), (ka_in, ka), (va_in, va), (do_in, do), (wq_in, wq))
        return [pltpu.make_async_copy(a.at[m], b.at[slot], l_sem.at[slot, n]) for n, (a, b) in enumerate(pairs)]

    extra = [pltpu.make_async_copy(x_in, x, c_sem.at[0]), pltpu.make_async_copy(gh_in, gh, c_sem.at[1])]
    for c in loads(0):
        c.start()
    for c in extra:
        c.start()
    greet([me.core, me.x, me.y, me.xy] + me.z[1:] + me.far)
    for unit in (ru, rd, ro, small_a):
        unit.stage(0)
    dw[...] = jnp.zeros_like(dw)
    small[...] = jnp.zeros_like(small)
    for m in range(groups):
        slot = m % 2
        if m + 1 < groups:
            for c in loads(m + 1):
                c.start()
        for c in loads(m):
            c.wait()
        dqt[...] = jnp.zeros_like(dqt)
        for h in range(3):
            base = 0 if h % 2 == 0 else HEAD_DIM
            flipped = jnp.transpose(ka[slot, h].astype(F32))
            kt[HEAD_DIM * h : HEAD_DIM * h + HEAD_DIM, :] = flipped[base : base + HEAD_DIM, :].astype(BF16)

        def block(i, carry, slot=slot):
            keys = pl.ds(pl.multiple_of(i * KEYS, KEYS), KEYS)
            dks, dvs = [], []
            for h in range(3):
                q = qa[slot, h]
                g = do[slot, h]
                p = jnp.exp(dot(ka[slot, h, keys, :], q, NT))
                dp = dot(va[slot, h, keys, :], g, NT)
                ds = (p * dp).astype(BF16)
                dvs.append(dot(p.astype(BF16), g, NN))
                dks.append(dot(ds, q, NN))
                mine = slice(HEAD_DIM * h, HEAD_DIM * h + HEAD_DIM)
                dqt[mine, :] += dot(kt[mine, keys], ds, NN)
            even = even_lanes((KEYS, 128))
            dk[keys, 0:128] = jnp.where(even, dks[0], dks[1])
            dk[keys, 128:256] = jnp.where(even, dks[2], 0.0)
            turned = [pltpu.roll(v, HEAD_DIM, 1) for v in dvs]
            dv[keys, 0:128] = jnp.where(even, turned[0], turned[1]).astype(BF16)
            dv[keys, 128:256] = turned[2].astype(BF16)
            return carry

        lax.fori_loop(0, total // KEYS, block, 0)
        pump("k", m)
        if m == 0:
            for c in extra:
                c.wait()

        def finish(i, carry, m=m, slot=slot):
            rows = row_block(i)
            cosine, sine = rotary(meta, tab, m, rows, ROWS)
            even = even_lanes((ROWS, 128))
            dq = jnp.transpose(dqt[:, rows]) * (HEAD_DIM**-0.5)
            grads = [[dq[:, :128], dq[:, 128:]], [dk[rows, :128], dk[rows, 128:]]]
            plain = [
                [g[p] * cosine[:, 128 * p : 128 * p + 128] - swap_halves(g[p]) * sine[:, 128 * p : 128 * p + 128] for p in range(2)]
                for g in grads
            ]
            r0 = pltpu.roll(plain[1][0], HEAD_DIM, 1)
            r1 = pltpu.roll(plain[1][1], HEAD_DIM, 1)
            flat = jnp.concatenate(
                [
                    plain[0][0].astype(BF16),
                    jnp.where(even, plain[0][1], r0).astype(BF16),
                    jnp.where(even, r0, r1).astype(BF16),
                    dv[rows, :192],
                ],
                axis=1,
            )
            acc = dot(flat, wq[slot], NT)
            if m == 0:
                zero = jnp.zeros((ROWS, 128), F32)
                angle = []
                for p in range(2):
                    odd_q = qa[slot, 1, rows, :].astype(F32) if p == 0 else zero
                    odd_k = ka[slot, 1, rows, :].astype(F32) if p == 0 else zero
                    q = jnp.where(even, qa[slot, 2 * p, rows, :].astype(F32), odd_q) * (HEAD_DIM**0.5)
                    k = jnp.where(even, ka[slot, 2 * p, rows, :].astype(F32), odd_k)
                    term = grads[0][p] * swap_halves(q) + grads[1][p] * swap_halves(k)
                    first = lanes(term.shape) % HEAD_DIM < HALF
                    angle.append(jnp.where(first, -term, term))
                angle = jnp.concatenate(angle, axis=1)
                for axis in range(2):
                    p = meta[rows, axis : axis + 1].astype(F32)
                    small[axis : axis + 1, 0:256] += jnp.sum(angle * p, axis=0, keepdims=True)
                small[2:3, 0:576] += jnp.sum(flat.astype(F32), axis=0, keepdims=True)
                dw[...] += dot(x[rows, :], flat, TN)
                scaled, _ = norm_rows(tok[rows, :].astype(F32))
                small[3:4, :] += jnp.sum(acc * scaled, axis=0, keepdims=True)
                small[4:5, :] += jnp.sum(acc, axis=0, keepdims=True)
            if m > 0:
                acc += gx[rows, :]
            if m == groups - 1:
                scaled, inverse = norm_rows(tok[rows, :].astype(F32))
                gtok[rows, :] = (gh[rows, :] + norm_back(acc, scaled, inverse, gain1)).astype(BF16)
            else:
                gx[rows, :] = acc
            return carry

        lax.fori_loop(0, steps, finish, 0)
        if m == 0:
            dwq[...] = dw[...].astype(BF16)
        pump("f", m)
    for c in finals:
        c.wait()
    mail.finish()


def back(groups, n_dp, tok, meta, gain1, tab, front_sums, qa, ka, va, do, x, gh, wq, du, dd, do_w):
    total, width = tok.shape
    sds = jax.ShapeDtypeStruct
    slot = pltpu.VMEM((2, 3, total, 128), BF16)
    extra = max(1, 2 * (n_dp // PEERS).bit_length() - 2)
    far = (n_dp // PEERS).bit_length() - 1

    def rooms(shape):
        r, c = shape
        return [
            pltpu.VMEM((r // 2, c), BF16), pltpu.VMEM((r // 2, c), BF16), pltpu.VMEM((3, r // 8, c), BF16),
            pltpu.VMEM((r, c), BF16),
        ]

    dq_shape = wq.shape[1:]
    cols = dq_shape[1] // 3
    return pl.pallas_call(
        functools.partial(back_body, groups),
        out_shape=[
            sds((total, width), BF16), sds((24, width), F32), sds(du.shape, BF16), sds(dd.shape, BF16),
            sds((cols, width), BF16), sds(dq_shape, BF16),
        ],
        in_specs=[VMEM] * 5 + [ANY] * 10,
        out_specs=[VMEM] * 2 + [ANY] * 4,
        scratch_shapes=[
            pltpu.VMEM(dq_shape, F32), pltpu.VMEM(dq_shape, BF16), pltpu.VMEM((8, width), F32),
            pltpu.VMEM((groups, 8, width), F32),
            slot, slot, slot, slot, pltpu.VMEM((2,) + wq.shape[1:], BF16), pltpu.VMEM((total, width), BF16),
            pltpu.VMEM((total, width), F32), pltpu.VMEM((total, width), F32),
            pltpu.VMEM((256, total), BF16), pltpu.VMEM((256, total), F32),
            pltpu.VMEM((total, 256), F32), pltpu.VMEM((total, 256), BF16),
        ]
        + rooms(du.shape) + rooms(dd.shape) + rooms(do_w.shape) + rooms(dq_shape)
        + [
            pltpu.VMEM((2, extra, du.shape[0] // 8, du.shape[1]), BF16),
            pltpu.VMEM((extra, do_w.shape[0] // 8, do_w.shape[1]), BF16),
            pltpu.VMEM((extra, dq_shape[0] // 8, dq_shape[1]), BF16),
            pltpu.VMEM((2, 1 + far, 8, width), F32), pltpu.VMEM((2, 4 + far, 8, width), F32),
            pltpu.SemaphoreType.DMA((2, 5)), pltpu.SemaphoreType.DMA((6,)), pltpu.SemaphoreType.DMA((4,)),
            pltpu.SemaphoreType.DMA((BACK_MESSAGES,)), pltpu.SemaphoreType.DMA((BACK_MESSAGES,)),
        ],
        compiler_params=pltpu.CompilerParams(
            vmem_limit_bytes=62 * 1024 * 1024, collective_id=1, has_side_effects=True
        ),
        name="back",
    )(tok, meta, gain1, tab, front_sums, qa, ka, va, do, x, gh, wq, du, dd, do_w)


def vectors_body(v, attn_gain, attn_shift, bias, freq, out_bias, mlp_gain, mlp_shift, up_bias, down_bias):
    cols = bias.shape[1]
    mlp_gain[...] = v[0, :]
    mlp_shift[...] = v[1, :]
    out_bias[...] = v[2, :]
    down_bias[...] = v[3, :]
    up_bias[...] = v[4, :]
    attn_gain[...] = v[19, :]
    attn_shift[...] = v[20, :]
    for n in range(3):
        bias[n : n + 1, :] = v[10:11, cols * n : cols * (n + 1)]
    first = [v[8:10, HEAD_DIM * n : HEAD_DIM * n + HALF] for n in range(cols // HEAD_DIM)]
    second = [v[8:10, HEAD_DIM * n + HALF : HEAD_DIM * (n + 1)] for n in range(cols // HEAD_DIM)]
    freq[...] = jnp.concatenate([a + b for a, b in zip(first, second)], axis=1)


def split_vectors(v, cols, units):
    width = v.shape[1]
    flat = lambda n: jax.ShapeDtypeStruct((n,), F32)
    return pl.pallas_call(
        vectors_body,
        out_shape=[
            flat(width), flat(width), jax.ShapeDtypeStruct((3, cols), F32), jax.ShapeDtypeStruct((2, cols // 2), F32),
            flat(width), flat(width), flat(width), flat(units), flat(width),
        ],
        in_specs=[VMEM],
        out_specs=[VMEM] * 9,
        name="vectors",
    )(v)


def body(
    n_dp, n_tensor, tokens, cotangent, kept_counts, patch_pos, attn_gain, attn_shift, qkv_weight, qkv_bias,
    rope_freq, out_weight, out_bias, mlp_gain, mlp_shift, up_weight, up_bias, down_weight, down_bias,
):
    width = tokens.shape[1]
    cols = qkv_weight.shape[2]
    groups = n_tensor
    wq = qkv_weight.reshape(width, 3 * cols)
    vectors = (qkv_bias, rope_freq, up_bias, attn_gain, attn_shift, out_bias, mlp_gain, mlp_shift, down_bias)
    qa, ka, va, do, block_out, gh, x, wq_all, tab, meta, dwo, dwu, dwd, sums = front(
        groups, tokens, patch_pos, kept_counts, vectors, cotangent, wq, out_weight, up_weight, down_weight,
    )
    res = back(
        groups, n_dp, tokens, meta, attn_gain, tab, sums, qa, ka, va, do, x, gh, wq_all, dwu, dwd, dwo
    )
    grad_tokens, sums, du, dd, do_w, dq = res
    d_again, d_ashift, d_bias, d_freq, d_ob, d_mgain, d_mshift, d_ub, d_db = split_vectors(
        sums, cols, up_weight.shape[1]
    )
    return (
        block_out, grad_tokens, d_again, d_ashift, dq.reshape(width, 3, cols).astype(F32), d_bias, d_freq,
        do_w.astype(F32), d_ob, d_mgain, d_mshift, du.astype(F32), d_ub, dd.astype(F32), d_db,
    )


def solution(mesh):
    return jax.shard_map(
        functools.partial(body, mesh.shape["dp"], mesh.shape["tensor"]),
        mesh=mesh,
        in_specs=(
            P("dp", None), P("dp", None), P("dp"), P(None, "dp"), P(), P(), P(None, None, "tensor"),
            P(None, "tensor"), P(None, "tensor"), P("tensor", None), P(), P(), P(), P(None, "tensor"),
            P("tensor"), P("tensor", None), P(),
        ),
        out_specs=(
            P("dp", None), P("dp", None), P(), P(), P(None, None, "tensor"), P(None, "tensor"),
            P(None, "tensor"), P("tensor", None), P(), P(), P(), P(None, "tensor"), P("tensor"),
            P("tensor", None), P(),
        ),
        check_vma=False,
    )
```

```python
import functools

import jax
import jax.numpy as jnp
from jax import lax
from jax.experimental import pallas as pl
from jax.experimental.pallas import tpu as pltpu
from jax.sharding import PartitionSpec as P

HEAD_DIM = 64
HALF = HEAD_DIM // 2
GRID_SIDE = 24
EPS = 1e-06
BIG = 1e30
F32 = jnp.float32
BF16 = jnp.bfloat16
NN = (((1,), (0,)), ((), ()))
NT = (((1,), (1,)), ((), ()))
TN = (((0,), (0,)), ((), ()))
VMEM = pl.BlockSpec(memory_space=pltpu.VMEM)
SMEM = pl.BlockSpec(memory_space=pltpu.SMEM)
ANY = pl.BlockSpec(memory_space=pl.ANY)
MESH = pl.DeviceIdType.MESH
TABLE_ROWS = 32
PEERS = 8
PARAMS = pltpu.CompilerParams(vmem_limit_bytes=60 * 1024 * 1024)


def dot(a, b, dims):
    return lax.dot_general(a, b, dims, preferred_element_type=F32)


def lanes(shape):
    return lax.broadcasted_iota(jnp.int32, shape, len(shape) - 1)


def norm_rows(values):
    center = values - jnp.mean(values, axis=-1, keepdims=True)
    inverse = lax.rsqrt(jnp.mean(center * center, axis=-1, keepdims=True) + EPS)
    return center * inverse, inverse


def norm_back(grad_out, scaled, inverse, gain):
    grad_scaled = grad_out * gain
    inner = jnp.mean(grad_scaled, axis=-1, keepdims=True)
    along = jnp.mean(grad_scaled * scaled, axis=-1, keepdims=True)
    return inverse * (grad_scaled - inner - scaled * along)


def swap_halves(u):
    first = lanes(u.shape) % HEAD_DIM < HALF
    return jnp.where(first, pltpu.roll(u, 128 - HALF, 1), pltpu.roll(u, HALF, 1))


def split3(v):
    high = v.astype(BF16)
    rest = v - high.astype(F32)
    mid = rest.astype(BF16)
    low = (rest - mid.astype(F32)).astype(BF16)
    return high, mid, low


def gelu_parts(v):
    x = jnp.abs(v) * 0.7071067811865476
    t = 1.0 / (1.0 + 0.3275911 * x)
    e = jnp.exp(-(x * x))
    poly = t * (
        0.254829592
        + t * (-0.284496736 + t * (1.421413741 + t * (-1.453152027 + t * 1.061405429)))
    )
    tail = 0.5 * poly * e
    phi = jnp.where(v >= 0, 1.0 - tail, tail)
    return phi, e * 0.3989422804014327


ROWS = 512
KEYS = 256


def even_lanes(shape):
    return lanes(shape) < HEAD_DIM


def rotary(meta, tab, m, rows, count):
    lane = lanes((count, 128))
    parts = []
    for axis in range(2):
        p = meta[rows, axis : axis + 1]
        hot = (lane == p) | (lane == p + TABLE_ROWS) | (lane == p + 2 * TABLE_ROWS)
        parts.append(dot(hot.astype(F32).astype(BF16), tab[m, axis], NN))
    rc, rs = parts[0][:, :256], parts[0][:, 256:]
    cc, sc = parts[1][:, :256], parts[1][:, 256:]
    cosine = rc * cc - rs * sc
    sine = rs * cc + rc * sc
    sine = jnp.where(lanes(sine.shape) % HEAD_DIM < HALF, -sine, sine)
    return cosine, sine


def as_row(ref):
    return ref[...].reshape(1, ref.shape[0])


def row_block(i):
    return pl.ds(pl.multiple_of(i * ROWS, ROWS), ROWS)


class Places:
    def __init__(self):
        d, t = lax.axis_index("dp"), lax.axis_index("tensor")
        self.d, self.t = d, t
        low = d % PEERS
        b0, b1, b2 = low % 2, (low // 2) % 2, low // 4
        core, across_x, across_y = 1 - 2 * b0, 2 - 4 * b1, 4 - 8 * b2
        t0, t1 = t % 2, (t // 2) % 2
        flip0, flip1 = 1 - 2 * t0, 2 - 4 * t1
        self.slice = low
        self.slice_x, self.slice_y = low + across_x, low + across_y
        self.slice_xy = low + across_x + across_y
        self.core_step = core
        self.half = b0
        self.core = (d + core, t)
        self.x = (d + across_x, t)
        self.y = (d + across_y, t)
        self.xy = (d + across_x + across_y, t)
        j, jx, jy = b1 + 2 * b2, 1 - 2 * b1, 2 - 4 * b2
        self.quarter, self.quarter_x, self.quarter_y, self.quarter_xy = j, j + jx, j + jy, j + jx + jy
        self.far = []
        step = PEERS
        while step < lax.axis_size("dp"):
            self.far.append((d + step - 2 * step * ((d // step) % 2), t))
            step *= 2
        self.z = [None, (d, t + flip0), (d, t + flip1), (d, t + flip0 + flip1)]


def greet(partners):
    barrier = pltpu.get_barrier_semaphore()
    for p in partners:
        pl.semaphore_signal(barrier, inc=1, device_id=p, device_id_type=MESH)
    pl.semaphore_wait(barrier, len(partners))


class Mail:
    def __init__(self, send_sem, recv_sem):
        self.send_sem, self.recv_sem = send_sem, recv_sem
        self.count = 0
        self.sent = []

    def number(self):
        self.count += 1
        return self.count - 1

    def send(self, n, src, dst, device):
        copy = pltpu.make_async_remote_copy(
            src_ref=src, dst_ref=dst, send_sem=self.send_sem.at[n], recv_sem=self.recv_sem.at[n],
            device_id=device, device_id_type=MESH,
        )
        copy.start()
        self.sent.append(copy)

    def arrive(self, n, dst, device):
        pltpu.make_async_remote_copy(
            src_ref=dst, dst_ref=dst, send_sem=self.send_sem.at[n], recv_sem=self.recv_sem.at[n],
            device_id=device, device_id_type=MESH,
        ).wait_recv()

    def finish(self):
        for copy in self.sent:
            copy.wait_send()


class Sliced:
    def __init__(self, mail, me, sources, targets, view, height):
        self.mail, self.me, self.view, self.height = mail, me, view, height
        self.transfers = targets
        self.z = [mail.number() for _ in targets]
        self.n = [mail.number() for _ in range(8)]

    def piece(self, s, off=0, size=None):
        size = self.height if size is None else size
        return self.view(pl.ds(pl.multiple_of(s * self.height + off, 16), size))

    def stage(self, k):
        mail, me, n = self.mail, self.me, self.n
        half = self.height // 2
        mine, sx, sy, sxy = me.slice, me.slice_x, me.slice_y, me.slice_xy
        if k == 0:
            for i, (device, source, landing) in zip(self.z, self.transfers):
                rows = pl.ds(pl.multiple_of(mine * self.height, 16), self.height)
                mail.send(i, source(rows), landing(rows), device)
        elif k == 1:
            for i, (device, source, landing) in zip(self.z, self.transfers):
                rows = pl.ds(pl.multiple_of(mine * self.height, 16), self.height)
                mail.arrive(i, landing(rows), device)
            mail.send(n[0], self.piece(mine), self.piece(mine), me.x)
            mail.send(n[1], self.piece(mine), self.piece(mine), me.y)
            mail.send(n[2], self.piece(mine), self.piece(mine), me.core)
        elif k == 2:
            mail.arrive(n[0], self.piece(sx), me.x)
            mail.send(n[3], self.piece(sx, 0, half), self.piece(sx, 0, half), me.y)
            mail.send(n[5], self.piece(sx), self.piece(sx), me.core)
            mail.arrive(n[1], self.piece(sy), me.y)
            mail.send(n[4], self.piece(sy, half, half), self.piece(sy, half, half), me.x)
            mail.send(n[6], self.piece(sy), self.piece(sy), me.core)
        elif k == 3:
            mail.arrive(n[3], self.piece(sxy, 0, half), me.y)
            mail.arrive(n[4], self.piece(sxy, half, half), me.x)
            mail.send(n[7], self.piece(sxy), self.piece(sxy), me.core)
        else:
            for i, s in ((2, mine), (5, sx), (6, sy), (7, sxy)):
                mail.arrive(n[i], self.piece(s + me.core_step), me.core)


class Direct:
    def __init__(self, mail, me, device, source, landing, height):
        self.mail, self.me = mail, me
        self.device, self.source, self.landing, self.height = device, source, landing, height
        self.n = [mail.number(), mail.number()]

    def stage(self, k):
        mail, me = self.mail, self.me
        mine = pl.ds(pl.multiple_of(me.half * self.height, 16), self.height)
        other = pl.ds(pl.multiple_of((1 - me.half) * self.height, 16), self.height)
        if k == 0:
            mail.send(self.n[0], self.source(mine), self.landing(mine), self.device)
        elif k == 1:
            mail.arrive(self.n[0], self.landing(mine), self.device)
            mail.send(self.n[1], self.landing(mine), self.landing(mine), me.core)
        else:
            mail.arrive(self.n[1], self.landing(other), me.core)


class Reduce:
    def __init__(self, mail, me, src, load_sem, came, own, parts, final, spare):
        self.mail, self.me, self.src, self.load_sem = mail, me, src, load_sem
        self.came, self.own, self.parts, self.final, self.spare = came, own, parts, final, spare
        self.half, self.quarter = own.shape[0], parts.shape[1]
        self.n = [mail.number() for _ in range(8 + len(me.far))]

    def band(self, start, size):
        return pl.ds(pl.multiple_of(start, 16), size)

    def load(self):
        mine = self.band(self.me.half * self.half, self.half)
        return pltpu.make_async_copy(self.src.at[mine, :], self.own, self.load_sem)

    def stage(self, k):
        mail, me, n = self.mail, self.me, self.n
        half, quarter = self.half, self.quarter
        places = ((me.x, me.quarter_x), (me.y, me.quarter_y), (me.xy, me.quarter_xy))
        spot = lambda j: self.final.at[self.band(me.half * half + j * quarter, quarter), :]
        if k == 0:
            self.load().start()
            other = self.band((1 - me.half) * half, half)
            mail.send(n[0], self.src.at[other, :], self.came, me.core)
        elif k == 1:
            self.load().wait()
            mail.arrive(n[0], self.came, me.core)
            self.own[...] = (self.own[...].astype(F32) + self.came[...].astype(F32)).astype(BF16)
            for i, (device, j) in enumerate(places):
                mail.send(n[1 + i], self.own.at[self.band(j * quarter, quarter), :], self.parts.at[i], device)
        elif k == 2:
            for i, (device, _) in enumerate(places):
                mail.arrive(n[1 + i], self.parts.at[i], device)
            total = self.own[self.band(me.quarter * quarter, quarter), :].astype(F32)
            for i in range(3):
                total += self.parts[i].astype(F32)
            for i, device in enumerate(me.far):
                self.spare[2 * i] = total.astype(BF16)
                mail.send(n[8 + i], self.spare.at[2 * i], self.spare.at[2 * i + 1], device)
                mail.arrive(n[8 + i], self.spare.at[2 * i + 1], device)
                total += self.spare[2 * i + 1].astype(F32)
            self.final[self.band(me.half * half + me.quarter * quarter, quarter), :] = total.astype(BF16)
            for i, (device, _) in enumerate(places):
                mail.send(n[4 + i], spot(me.quarter), spot(me.quarter), device)
        elif k == 3:
            for i, (device, j) in enumerate(places):
                mail.arrive(n[4 + i], spot(j), device)
            mine = self.final.at[self.band(me.half * half, half), :]
            mail.send(n[7], mine, mine, me.core)
        else:
            mail.arrive(n[7], self.final.at[self.band((1 - me.half) * half, half), :], me.core)


class ReduceSmall:
    def __init__(self, mail, me, src, hold, came):
        self.mail, self.me, self.src, self.hold, self.came = mail, me, src, hold, came
        self.n = [mail.number() for _ in range(4 + len(me.far))]

    def stage(self, k):
        mail, me, n = self.mail, self.me, self.n
        places = (me.x, me.y, me.xy)
        if k == 0:
            mail.send(n[0], self.src, self.came.at[0], me.core)
        elif k == 1:
            mail.arrive(n[0], self.came.at[0], me.core)
            self.hold[0] = self.src[...] + self.came[0]
            for i, device in enumerate(places):
                mail.send(n[1 + i], self.hold.at[0], self.came.at[1 + i], device)
        else:
            for i, device in enumerate(places):
                mail.arrive(n[1 + i], self.came.at[1 + i], device)
            total = (self.hold[0] + self.came[1]) + (self.came[2] + self.came[3])
            for i, device in enumerate(me.far):
                self.hold[1 + i] = total
                mail.send(n[4 + i], self.hold.at[1 + i], self.came.at[4 + i], device)
                mail.arrive(n[4 + i], self.came.at[4 + i], device)
                total = total + self.came[4 + i]
            return total


class Scatter:
    def __init__(self, mail, me, grad, came, parts, piece, spare):
        self.mail, self.me, self.grad, self.came, self.parts = mail, me, grad, came, parts
        self.piece, self.spare = piece, spare
        self.half, self.quarter = came.shape[0], parts.shape[1]
        self.n = [mail.number() for _ in range(4 + len(me.far))]

    def band(self, start, size):
        return pl.ds(pl.multiple_of(start, 16), size)

    def stage(self, k):
        mail, me, n = self.mail, self.me, self.n
        half, quarter = self.half, self.quarter
        places = ((me.x, me.quarter_x), (me.y, me.quarter_y), (me.xy, me.quarter_xy))
        if k == 0:
            mail.send(n[0], self.grad.at[self.band((1 - me.half) * half, half), :], self.came, me.core)
        elif k == 1:
            mail.arrive(n[0], self.came, me.core)
            mine = self.grad[self.band(me.half * half, half), :]
            self.came[...] = (mine.astype(F32) + self.came[...].astype(F32)).astype(BF16)
            for i, (device, j) in enumerate(places):
                mail.send(n[1 + i], self.came.at[self.band(j * quarter, quarter), :], self.parts.at[i], device)
        else:
            for i, (device, _) in enumerate(places):
                mail.arrive(n[1 + i], self.parts.at[i], device)
            total = self.came[self.band(me.quarter * quarter, quarter), :].astype(F32)
            for i in range(3):
                total += self.parts[i].astype(F32)
            for i, device in enumerate(me.far):
                self.parts[i] = total.astype(BF16)
                mail.send(n[4 + i], self.parts.at[i], self.spare.at[i], device)
                mail.arrive(n[4 + i], self.spare.at[i], device)
                total += self.spare[i].astype(F32)
            self.piece[...] = total.astype(BF16)


class Spread:
    def __init__(self, mail, me, piece, load_sem, final):
        self.mail, self.me, self.piece, self.load_sem, self.final = mail, me, piece, load_sem, final
        self.quarter = piece.shape[0]
        self.n = [mail.number() for _ in range(4)]

    def band(self, start, size):
        return self.final.at[pl.ds(pl.multiple_of(start, 16), size), :]

    def stage(self, k):
        mail, me, n, quarter = self.mail, self.me, self.n, self.quarter
        half = 4 * quarter
        places = ((me.x, me.quarter_x), (me.y, me.quarter_y), (me.xy, me.quarter_xy))
        spot = lambda j: self.band(me.half * half + j * quarter, quarter)
        if k == 0:
            load = pltpu.make_async_copy(self.piece, spot(me.quarter), self.load_sem)
            load.start()
            load.wait()
            for i, (device, _) in enumerate(places):
                mail.send(n[i], spot(me.quarter), spot(me.quarter), device)
        elif k == 3:
            for i, (device, j) in enumerate(places):
                mail.arrive(n[i], spot(j), device)
            mine = self.band(me.half * half, half)
            mail.send(n[3], mine, mine, me.core)
        else:
            mail.arrive(n[3], self.band((1 - me.half) * half, half), me.core)


FRONT_MESSAGES = 96


def front_body(
    groups, tok, posr, counts, bias, freq, up_bias, gain1, shift1, ob, gain2, shift2, db,
    cot_in, wq_in, wo_in, wu_in, wd_in,
    qa_out, ka_out, va_out, do_out, out_out, gh_out, x_out, wq_out, tab_out, meta, dwo, piece_u, piece_d, sums,
    part_u, part_d, dwu, dwd, came_u, came_d, parts_u, parts_d, spare, wq, wo, wud, pk, tab, flipped, cot, x, qa, ka, va, mixed, hidden, x2, unit_acc, grad_acc, dos,
    w_sem, s_sem, o_sem, e_sem, send_sem, recv_sem,
):
    total = tok.shape[0]
    cols = wo_in.shape[0]
    width = tok.shape[1]
    steps = total // ROWS
    me = Places()
    mail = Mail(send_sem, recv_sem)
    lift = 256 - cols
    gain1, shift1, ob, gain2, shift2, db = (as_row(v) for v in (gain1, shift1, ob, gain2, shift2, db))
    loads = [
        pltpu.make_async_copy(wq_in, wq.at[0], w_sem.at[0]),
        pltpu.make_async_copy(cot_in, cot, w_sem.at[1]),
        pltpu.make_async_copy(wo_in, wo.at[0, pl.ds(lift, cols), :], w_sem.at[2]),
        pltpu.make_async_copy(wu_in, wud.at[0, 0], w_sem.at[3]),
        pltpu.make_async_copy(wd_in, wud.at[0, 1], w_sem.at[4]),
    ]
    for c in loads:
        c.start()
    pack_numbers = [mail.number() for _ in range(groups - 1)]
    q1 = Direct(mail, me, me.z[1], lambda r: wq_in.at[r, :], lambda r: wq.at[1, r, :], width // 2)
    qh = width // PEERS
    qn = {
        m: Sliced(
            mail, me, None, [(me.z[m], lambda r: wq_in.at[r, :], lambda r, m=m: wq.at[m, r, :])],
            lambda r, m=m: wq.at[m, r, :], qh,
        )
        for m in range(2, groups)
    }
    oc = Sliced(
        mail, me, None,
        [(me.z[m], lambda r: wo.at[0, r, :], lambda r, m=m: wo.at[m, r, :]) for m in range(1, groups)],
        lambda r: wo.at[pl.ds(1, groups - 1), r, :], 256 // PEERS,
    )
    ud = {
        m: Sliced(
            mail, me, None,
            [
                (me.z[m], lambda r: wu_in.at[r, :], lambda r, m=m: wud.at[m, 0, r, :]),
                (me.z[m], lambda r: wd_in.at[r, :], lambda r, m=m: wud.at[m, 1, r, :]),
            ],
            lambda r, m=m: wud.at[m, :, r, :], width // PEERS,
        )
        for m in range(1, groups)
    }
    ru = Scatter(mail, me, dwu, came_u, parts_u, piece_u, spare.at[0])
    rd = Scatter(mail, me, dwd, came_d, parts_d, piece_d, spare.at[1])
    wo[0, 0:lift, :] = jnp.zeros((lift, width), BF16)
    pk[0] = jnp.zeros((8, width), F32)
    pk[0, 0:1, :] = as_row(up_bias)
    pk[0, 1:2, 0 : 3 * cols] = jnp.concatenate([bias[n : n + 1, :] for n in range(3)], axis=1)
    by_lane = [freq[:, HALF * (n // 2) : HALF * (n // 2) + HALF] for n in range(2 * (cols // HEAD_DIM))]
    pk[0, 2:4, 0:cols] = jnp.concatenate(by_lane, axis=1)
    greet(me.z[1:] + [me.core, me.x, me.y, me.xy] + me.far)
    for m in range(1, groups):
        mail.send(pack_numbers[m - 1], pk.at[0], pk.at[m], me.z[m])
    q1.stage(0)

    flipped[...] = jnp.zeros_like(flipped)
    flipped[0:2, :] = posr[...].astype(F32)
    place = lax.broadcasted_iota(jnp.int32, (total, 8), 0)
    end = counts[0]
    segment = (place >= end).astype(jnp.int32)
    for n in range(1, counts.shape[0]):
        end = end + counts[n]
        segment += (place >= end).astype(jnp.int32)
    alive = (place < end).astype(jnp.int32)
    lane8 = lanes((total, 8))
    meta[...] = jnp.where(
        lane8 == 2, segment, jnp.where(lane8 == 3, alive, jnp.transpose(flipped[...]).astype(jnp.int32))
    )

    def make_table(m):
        place = lax.broadcasted_iota(jnp.int32, (TABLE_ROWS, 256), 0).astype(F32)
        for axis in range(2):
            angle = place * pk[m, 2 + axis : 3 + axis, 0:256]
            for n, part in enumerate(split3(jnp.concatenate([jnp.cos(angle), jnp.sin(angle)], axis=1))):
                tab[m, axis, TABLE_ROWS * n : TABLE_ROWS * (n + 1), :] = part
            tab[m, axis, 3 * TABLE_ROWS :, :] = jnp.zeros((128 - 3 * TABLE_ROWS, 512), BF16)

    plan = {
        ("n", 0, 1): [(qn[2], 0), (qn[3], 0)],
        ("a", 0, 1): [(q1, 1), (qn[2], 1), (qn[3], 1), (ud[1], 0), (oc, 0), (ud[2], 0), (q1, 2)],
        ("p", 1, 1): [(qn[2], 2)],
        ("a", 1, 0): [(qn[2], 3), (qn[3], 2)],
        ("a", 1, 1): [(ud[3], 0), (qn[3], 3), (qn[2], 4)],
        ("p", 2, 1): [(oc, 1), (qn[3], 4)],
        ("a", 2, 0): [(oc, 2)],
        ("a", 2, 1): [(oc, 3), (ud[1], 1)],
        ("p", 3, 1): [(oc, 4)],
        ("a", 3, 1): [(ud[1], 2), (ud[2], 1)],
        ("h", 0, 1): [(ud[1], 3)],
        ("u", 0, 0): [(ud[2], 2), (ud[3], 1)],
        ("u", 0, 1): [(ud[1], 4), (ud[2], 3)],
        ("u", 1, 0): [(ud[3], 2), (ru, 0), (rd, 0)],
        ("u", 1, 1): [(ud[2], 4), (ud[3], 3)],
        ("u", 2, 1): [(ud[3], 4), (ru, 1), (rd, 1)],
        ("g", 0, 1): [(ru, 2), (rd, 2)],
    }

    def pump(*key):
        for what, k in plan.get(key, ()):
            what.stage(k)

    make_table(0)
    for i in range(steps):
        rows = pl.ds(i * ROWS, ROWS)
        scaled, _ = norm_rows(tok[rows, :].astype(F32))
        x[rows, :] = (scaled * gain1 + shift1).astype(BF16)
        pump("n", 0, i)
    x_store = pltpu.make_async_copy(x, x_out, s_sem.at[0, 3])
    x_store.start()

    def saves(m, slot):
        return [
            pltpu.make_async_copy(a.at[slot], b.at[m], s_sem.at[slot, n])
            for n, (a, b) in enumerate(((qa, qa_out), (ka, ka_out), (va, va_out)))
        ]

    def project(m, slot, i):
        rows = pl.ds(i * ROWS, ROWS)
        proj = dot(x[rows, :], wq[m], NN) + pk[m, 1:2, 0:576]
        cosine, sine = rotary(meta, tab, m, rows, ROWS)
        lane = lanes((ROWS, 128))
        even = lane < HEAD_DIM
        odd = jnp.logical_not(even)
        s = meta[rows, 2:3]
        r1 = pltpu.roll(proj[:, 128:256], HEAD_DIM, 1)
        r2 = pltpu.roll(proj[:, 256:384], HEAD_DIM, 1)
        rv = pltpu.roll(proj[:, 384:512], HEAD_DIM, 1)
        v_last = jnp.concatenate([jnp.ones((ROWS, HEAD_DIM), F32), proj[:, 512:576]], axis=1)
        qs = [proj[:, 0:128], proj[:, 128:256]]
        ks = [jnp.where(even, r1, r2), r2]
        for pair in range(2):
            sl = slice(128 * pair, 128 * pair + 128)
            c, sg = cosine[:, sl], sine[:, sl]
            qr = (qs[pair] * c + swap_halves(qs[pair]) * sg) * (HEAD_DIM**-0.5)
            kr = ks[pair] * c + swap_halves(ks[pair]) * sg
            for h in (0, 1) if pair == 0 else (2,):
                inside = even if h % 2 == 0 else odd
                j = lane - (HEAD_DIM if h % 2 == 0 else 0)
                fq = jnp.where((j < 3) & (j != s), -BIG, 0.0)
                fk = jnp.where((j == s) | ((j >= 3) & (j < 6)), 1.0, 0.0)
                qa[slot, h, rows, :] = jnp.where(inside, qr, fq).astype(BF16)
                ka[slot, h, rows, :] = jnp.where(inside, kr, fk).astype(BF16)
        va[slot, 0, rows, :] = jnp.where(even, 1.0, rv).astype(BF16)
        va[slot, 1, rows, :] = jnp.where(even, rv, 1.0).astype(BF16)
        va[slot, 2, rows, :] = v_last.astype(BF16)

    def attend(m, slot, i):
        rows = pl.ds(i * ROWS, ROWS)
        lane = lanes((ROWS, 128))
        outs = []
        for h in range(3):
            q = qa[slot, h, rows, :]
            s = dot(q, ka[slot, h], NT)
            peak = jnp.max(s, axis=1, keepdims=True)
            p = jnp.exp(s - peak).astype(BF16)
            o = dot(p, va[slot, h], NN)
            spot = 0 if h % 2 == 0 else HEAD_DIM
            base = HEAD_DIM if h % 2 == 0 else 0
            outs.append(o / pltpu.roll(o, HEAD_DIM, 1))
            high, mid, low = split3(-(peak + jnp.log(o[:, spot : spot + 1])))
            qn_ = q.astype(F32)
            qn_ = jnp.where(lane == base + 3, high.astype(F32), qn_)
            qn_ = jnp.where(lane == base + 4, mid.astype(F32), qn_)
            qn_ = jnp.where(lane == base + 5, low.astype(F32), qn_)
            qa[slot, h, rows, :] = qn_.astype(BF16)
        even = lane < HEAD_DIM
        mixed[m, rows, 0:128] = jnp.where(even, 0.0, outs[0]).astype(BF16)
        mixed[m, rows, 128:256] = jnp.where(even, outs[1], outs[2]).astype(BF16)

    loads[0].wait()
    loads[2].wait()
    for m in range(groups):
        slot = m % 2
        if m >= 2:
            for c in saves(m - 2, slot):
                c.wait()
        for i in range(steps):
            project(m, slot, i)
            pump("p", m, i)
        for i in range(steps):
            attend(m, slot, i)
            if m == 0 and i == steps - 1:
                for n in range(1, groups):
                    mail.arrive(pack_numbers[n - 1], pk.at[n], me.z[n])
                    make_table(n)
            pump("a", m, i)
        for c in saves(m, slot):
            c.start()
    kept = [pltpu.make_async_copy(wq, wq_out, o_sem.at[3]), pltpu.make_async_copy(tab, tab_out, o_sem.at[4])]
    for c in kept:
        c.start()
    for c in loads[1:2] + loads[3:]:
        c.wait()

    for i in range(steps):
        rows = pl.ds(i * ROWS, ROWS)
        head_sum = dot(mixed[0, rows, :], wo[0], NN)
        for m in range(1, groups):
            head_sum += dot(mixed[m, rows, :], wo[m], NN)
        h = tok[rows, :].astype(F32) + head_sum + ob
        hidden[rows, :] = h
        scaled, _ = norm_rows(h)
        x2[rows, :] = (scaled * gain2 + shift2).astype(BF16)
        live = (meta[rows, 3:4]).astype(F32)
        cot[rows, :] = (cot[rows, :].astype(F32) * live).astype(BF16)
        pump("h", 0, i)
    sums[...] = jnp.zeros_like(sums)
    for m in range(groups):
        for i in range(steps):
            rows = pl.ds(i * ROWS, ROWS)
            xr = x2[rows, :]
            gr = cot[rows, :]
            upward = dot(xr, wud[m, 0], NN) + pk[m, 0:1, :]
            grad_activ = dot(gr, wud[m, 1], NT)
            phi, density = gelu_parts(upward)
            activ = (upward * phi).astype(BF16)
            grad_up = (grad_activ * (phi + upward * density)).astype(BF16)
            unit = dot(activ, wud[m, 1], NN)
            grad_in = dot(grad_up, wud[m, 0], NT)
            if m == 0:
                unit_acc[rows, :] = unit
                grad_acc[rows, :] = grad_in
                down, up = dot(activ, gr, TN), dot(xr, grad_up, TN)
                if i > 0:
                    down, up = part_d[...] + down, part_u[...] + up
                if i < steps - 1:
                    part_d[...], part_u[...] = down, up
                else:
                    dwd[...], dwu[...] = down.astype(BF16), up.astype(BF16)
                sums[4:5, :] += jnp.sum(grad_up.astype(F32), axis=0, keepdims=True)
            else:
                unit_acc[rows, :] += unit
                grad_acc[rows, :] += grad_in
            pump("u", m, i)
    x_store.wait()
    last = []
    for i in range(steps):
        rows = pl.ds(i * ROWS, ROWS)
        h = hidden[rows, :]
        live = (meta[rows, 3:4]).astype(F32)
        x2[rows, :] = (live * (h + unit_acc[rows, :] + db)).astype(BF16)
        scaled, inverse = norm_rows(h)
        grad_result = cot[rows, :].astype(F32)
        grad_x = grad_acc[rows, :]
        grad_hidden = grad_result + norm_back(grad_x, scaled, inverse, gain2)
        hidden[rows, :] = grad_hidden
        low = grad_hidden.astype(BF16)
        sums[0:1, :] += jnp.sum(grad_x * scaled, axis=0, keepdims=True)
        sums[1:2, :] += jnp.sum(grad_x, axis=0, keepdims=True)
        sums[2:3, :] += jnp.sum(grad_hidden, axis=0, keepdims=True)
        sums[3:4, :] += jnp.sum(grad_result, axis=0, keepdims=True)
        part = dot(mixed[0, rows, :], low, TN)
        if i > 0:
            part += part_d[0:256, :]
        if i < steps - 1:
            part_d[0:256, :] = part
        else:
            dwo[...] = part.astype(BF16)
        lane = lanes((ROWS, 128))
        even = lane < HEAD_DIM
        for m in range(groups):
            grad_mixed = dot(low, wo[m], NT).astype(BF16).astype(F32)
            for head in range(3):
                sl = slice(0, 128) if head == 0 else slice(128, 256)
                product = grad_mixed[:, sl] * mixed[m, rows, sl].astype(F32)
                inside = even if head % 2 == 1 else jnp.logical_not(even)
                base = 0 if head % 2 == 0 else HEAD_DIM
                inner = jnp.sum(jnp.where(inside, product, 0.0), axis=1, keepdims=True)
                high, mid, lo = split3(-inner)
                value = jnp.where(inside, grad_mixed[:, sl], 0.0)
                value = jnp.where(lane == base, high.astype(F32), value)
                value = jnp.where(lane == base + 1, mid.astype(F32), value)
                value = jnp.where(lane == base + 2, lo.astype(F32), value)
                dos[m, head, rows, :] = value.astype(BF16)
        block = [
            pltpu.make_async_copy(dos.at[:, :, rows, :], do_out.at[:, :, rows, :], e_sem.at[i, 0]),
            pltpu.make_async_copy(x2.at[rows, :], out_out.at[rows, :], e_sem.at[i, 1]),
            pltpu.make_async_copy(hidden.at[rows, :], gh_out.at[rows, :], e_sem.at[i, 2]),
        ]
        for c in block:
            c.start()
        last += block
        pump("g", 0, i)
    for m in range(max(groups - 2, 0), groups):
        for c in saves(m, m % 2):
            c.wait()
    for c in last + kept:
        c.wait()
    mail.finish()


def front(groups, n_dp, tok, posr, counts, vectors, cot, wq, wo, wu, wd):
    total, width = tok.shape
    units = wu.shape[1]
    far = (n_dp // PEERS).bit_length() - 1
    sds = jax.ShapeDtypeStruct
    heads = sds((groups, 3, total, 128), BF16)
    outs = [heads] * 4 + [
        sds((total, width), BF16), sds((total, width), F32), sds((total, width), BF16),
        sds((groups,) + wq.shape, BF16), sds((groups, 2, 128, 512), BF16), sds((total, 8), jnp.int32),
        sds((256, width), BF16), sds((width // 8, units), BF16), sds((units // 8, width), BF16), sds((8, width), F32),
    ]
    slot = pltpu.VMEM((2, 3, total, 128), BF16)
    rowsb = pltpu.VMEM((total, width), BF16)
    rowsf = pltpu.VMEM((total, width), F32)
    return pl.pallas_call(
        functools.partial(front_body, groups),
        out_shape=outs,
        in_specs=[VMEM] * 2 + [SMEM] + [VMEM] * len(vectors) + [ANY] * 5,
        out_specs=[ANY] * 9 + [VMEM] * 5,
        scratch_shapes=[
            pltpu.VMEM((width, units), F32), pltpu.VMEM((units, width), F32),
            pltpu.VMEM((width, units), BF16), pltpu.VMEM((units, width), BF16),
            pltpu.VMEM((width // 2, units), BF16), pltpu.VMEM((units // 2, width), BF16),
            pltpu.VMEM((3, width // 8, units), BF16), pltpu.VMEM((3, units // 8, width), BF16),
            pltpu.VMEM((2, max(1, far), width // 8, units), BF16),
            pltpu.VMEM((groups,) + wq.shape, BF16), pltpu.VMEM((groups, 256, width), BF16),
            pltpu.VMEM((groups, 2, width, units), BF16), pltpu.VMEM((groups, 8, width), F32),
            pltpu.VMEM((groups, 2, 128, 512), BF16), pltpu.VMEM((8, total), F32),
            rowsb, rowsb, slot, slot, slot,
            pltpu.VMEM((groups, total, 256), BF16), rowsf, rowsb, rowsf, rowsf,
            pltpu.VMEM((groups, 3, total, 128), BF16),
            pltpu.SemaphoreType.DMA((5,)), pltpu.SemaphoreType.DMA((2, 4)), pltpu.SemaphoreType.DMA((5,)),
            pltpu.SemaphoreType.DMA((total // ROWS, 3)),
            pltpu.SemaphoreType.DMA((FRONT_MESSAGES,)), pltpu.SemaphoreType.DMA((FRONT_MESSAGES,)),
        ],
        compiler_params=pltpu.CompilerParams(
            vmem_limit_bytes=62 * 1024 * 1024, collective_id=0, has_side_effects=True
        ),
        name="front",
    )(tok, posr, counts, *vectors, cot, wq, wo, wu, wd)


BACK_MESSAGES = 64


def back_body(
    groups, tok_in, meta, gain1, tab, front_sums, qa_in, ka_in, va_in, do_in, x_in, gh_in, wq_in, du_in, dd_in, do_w_in,
    gtok, vectors, du_out, dd_out, do_w_out, dq_out,
    tok, dw, dwq, small, across, qa, ka, va, do, wq, x, gh, gx, kt, dqt, dk, dv,
    final_u, final_d, came_o, own_o, parts_o, final_o,
    came_q, own_q, parts_q, final_q, spare_o, spare_q, hold, came_s,
    l_sem, c_sem, r_sem, send_sem, recv_sem,
):
    total = tok_in.shape[0]
    steps = total // ROWS
    me = Places()
    mail = Mail(send_sem, recv_sem)
    gain1 = as_row(gain1)
    cols = wq_in.shape[2] // 3
    across_numbers = [mail.number() for _ in range(groups - 1)]
    ru = Spread(mail, me, du_in, r_sem.at[0], final_u)
    rd = Spread(mail, me, dd_in, r_sem.at[1], final_d)
    ro = Reduce(mail, me, do_w_in, r_sem.at[2], came_o, own_o, parts_o, final_o, spare_o)
    rq = Reduce(mail, me, dwq, r_sem.at[3], came_q, own_q, parts_q, final_q, spare_q)
    small_a = ReduceSmall(mail, me, front_sums, hold.at[0], came_s.at[0])
    small_b = ReduceSmall(mail, me, small, hold.at[1], came_s.at[1])
    finals = [
        pltpu.make_async_copy(a, b, c_sem.at[2 + n])
        for n, (a, b) in enumerate(((final_u, du_out), (final_d, dd_out), (final_o.at[256 - cols :, :], do_w_out), (final_q, dq_out)))
    ]
    plan = {
        ("k", 0): [(ro, 1), (small_a, 1)],
        ("f", 0): [(rq, 0), (small_b, 0)],
        ("k", 1): [(ru, 3), (rd, 3), (ro, 2), (rq, 1), (small_a, 2), (small_b, 1)],
        ("f", 1): [(ru, 4), (rd, 4)],
        ("k", 2): [(ro, 3), (rq, 2), (small_b, 2)],
        ("f", 2): [(ro, 4)],
        ("k", 3): [(rq, 3), (small_b, 3)],
        ("f", 3): [(rq, 4)],
    }

    def pump(*key):
        for what, k in plan.get(key, ()):
            if what is small_b and k == 3:
                for n in range(1, groups):
                    mail.arrive(across_numbers[n - 1], across.at[n], me.z[n])
                total = (across[0] + across[1]) + (across[2] + across[3])
                vectors[16:24, :] = total
                continue
            value = what.stage(k)
            if what is small_a and k == 2:
                vectors[0:8, :] = value
            if what is small_b and k == 2:
                across[0] = value
                for n in range(1, groups):
                    mail.send(across_numbers[n - 1], across.at[0], across.at[n], me.z[n])
                vectors[8:16, :] = value
            for n, unit in enumerate((ru, rd, ro, rq)):
                if what is unit and k == 4:
                    finals[n].start()

    def loads(m):
        slot = m % 2
        pairs = ((qa_in, qa), (ka_in, ka), (va_in, va), (do_in, do), (wq_in, wq))
        return [pltpu.make_async_copy(a.at[m], b.at[slot], l_sem.at[slot, n]) for n, (a, b) in enumerate(pairs)]

    extra = [pltpu.make_async_copy(x_in, x, c_sem.at[0]), pltpu.make_async_copy(gh_in, gh, c_sem.at[1])]
    extra.append(pltpu.make_async_copy(tok_in, tok, c_sem.at[6]))
    for c in loads(0):
        c.start()
    for c in extra:
        c.start()
    greet([me.core, me.x, me.y, me.xy] + me.z[1:] + me.far)
    for unit in (ru, rd, ro, small_a):
        unit.stage(0)
    dw[...] = jnp.zeros_like(dw)
    small[...] = jnp.zeros_like(small)
    for m in range(groups):
        slot = m % 2
        if m + 1 < groups:
            for c in loads(m + 1):
                c.start()
        for c in loads(m):
            c.wait()
        dqt[...] = jnp.zeros_like(dqt)
        for h in range(3):
            base = 0 if h % 2 == 0 else HEAD_DIM
            flipped = jnp.transpose(ka[slot, h].astype(F32))
            kt[HEAD_DIM * h : HEAD_DIM * h + HEAD_DIM, :] = flipped[base : base + HEAD_DIM, :].astype(BF16)

        def block(i, carry, slot=slot):
            keys = pl.ds(pl.multiple_of(i * KEYS, KEYS), KEYS)
            dks, dvs = [], []
            for h in range(3):
                q = qa[slot, h]
                g = do[slot, h]
                p = jnp.exp(dot(ka[slot, h, keys, :], q, NT))
                dp = dot(va[slot, h, keys, :], g, NT)
                ds = (p * dp).astype(BF16)
                dvs.append(dot(p.astype(BF16), g, NN))
                dks.append(dot(ds, q, NN))
                mine = slice(HEAD_DIM * h, HEAD_DIM * h + HEAD_DIM)
                dqt[mine, :] += dot(kt[mine, keys], ds, NN)
            even = even_lanes((KEYS, 128))
            dk[keys, 0:128] = jnp.where(even, dks[0], dks[1])
            dk[keys, 128:256] = jnp.where(even, dks[2], 0.0)
            turned = [pltpu.roll(v, HEAD_DIM, 1) for v in dvs]
            dv[keys, 0:128] = jnp.where(even, turned[0], turned[1]).astype(BF16)
            dv[keys, 128:256] = turned[2].astype(BF16)
            return carry

        lax.fori_loop(0, total // KEYS, block, 0)
        pump("k", m)
        if m == 0:
            for c in extra:
                c.wait()

        def finish(i, carry, m=m, slot=slot):
            rows = row_block(i)
            cosine, sine = rotary(meta, tab, m, rows, ROWS)
            even = even_lanes((ROWS, 128))
            dq = jnp.transpose(dqt[:, rows]) * (HEAD_DIM**-0.5)
            grads = [[dq[:, :128], dq[:, 128:]], [dk[rows, :128], dk[rows, 128:]]]
            plain = [
                [g[p] * cosine[:, 128 * p : 128 * p + 128] - swap_halves(g[p]) * sine[:, 128 * p : 128 * p + 128] for p in range(2)]
                for g in grads
            ]
            r0 = pltpu.roll(plain[1][0], HEAD_DIM, 1)
            r1 = pltpu.roll(plain[1][1], HEAD_DIM, 1)
            flat = jnp.concatenate(
                [
                    plain[0][0].astype(BF16),
                    jnp.where(even, plain[0][1], r0).astype(BF16),
                    jnp.where(even, r0, r1).astype(BF16),
                    dv[rows, :192],
                ],
                axis=1,
            )
            acc = dot(flat, wq[slot], NT)
            if m == 0:
                zero = jnp.zeros((ROWS, 128), F32)
                angle = []
                for p in range(2):
                    odd_q = qa[slot, 1, rows, :].astype(F32) if p == 0 else zero
                    odd_k = ka[slot, 1, rows, :].astype(F32) if p == 0 else zero
                    q = jnp.where(even, qa[slot, 2 * p, rows, :].astype(F32), odd_q) * (HEAD_DIM**0.5)
                    k = jnp.where(even, ka[slot, 2 * p, rows, :].astype(F32), odd_k)
                    term = grads[0][p] * swap_halves(q) + grads[1][p] * swap_halves(k)
                    first = lanes(term.shape) % HEAD_DIM < HALF
                    angle.append(jnp.where(first, -term, term))
                angle = jnp.concatenate(angle, axis=1)
                for axis in range(2):
                    p = meta[rows, axis : axis + 1].astype(F32)
                    small[axis : axis + 1, 0:256] += jnp.sum(angle * p, axis=0, keepdims=True)
                small[2:3, 0:576] += jnp.sum(flat.astype(F32), axis=0, keepdims=True)
                dw[...] += dot(x[rows, :], flat, TN)
                scaled, _ = norm_rows(tok[rows, :].astype(F32))
                small[3:4, :] += jnp.sum(acc * scaled, axis=0, keepdims=True)
                small[4:5, :] += jnp.sum(acc, axis=0, keepdims=True)
            if m > 0:
                acc += gx[rows, :]
            if m == groups - 1:
                scaled, inverse = norm_rows(tok[rows, :].astype(F32))
                gtok[rows, :] = (gh[rows, :] + norm_back(acc, scaled, inverse, gain1)).astype(BF16)
            else:
                gx[rows, :] = acc
            return carry

        lax.fori_loop(0, steps, finish, 0)
        if m == 0:
            dwq[...] = dw[...].astype(BF16)
        pump("f", m)
    for c in finals:
        c.wait()
    mail.finish()


def back(groups, n_dp, tok, meta, gain1, tab, front_sums, qa, ka, va, do, x, gh, wq, du, dd, do_w):
    total, width = tok.shape
    sds = jax.ShapeDtypeStruct
    slot = pltpu.VMEM((2, 3, total, 128), BF16)
    extra = max(1, 2 * (n_dp // PEERS).bit_length() - 2)
    far = (n_dp // PEERS).bit_length() - 1

    def rooms(shape):
        r, c = shape
        return [
            pltpu.VMEM((r // 2, c), BF16), pltpu.VMEM((r // 2, c), BF16), pltpu.VMEM((3, r // 8, c), BF16),
            pltpu.VMEM((r, c), BF16),
        ]

    dq_shape = wq.shape[1:]
    du_shape, dd_shape = (8 * du.shape[0], du.shape[1]), (8 * dd.shape[0], dd.shape[1])
    cols = dq_shape[1] // 3
    return pl.pallas_call(
        functools.partial(back_body, groups),
        out_shape=[
            sds((total, width), BF16), sds((24, width), F32), sds(du_shape, BF16), sds(dd_shape, BF16),
            sds((cols, width), BF16), sds(dq_shape, BF16),
        ],
        in_specs=[ANY] + [VMEM] * 4 + [ANY] * 10,
        out_specs=[VMEM] * 2 + [ANY] * 4,
        scratch_shapes=[
            pltpu.VMEM((total, width), BF16), pltpu.VMEM(dq_shape, F32), pltpu.VMEM(dq_shape, BF16), pltpu.VMEM((8, width), F32),
            pltpu.VMEM((groups, 8, width), F32),
            slot, slot, slot, slot, pltpu.VMEM((2,) + wq.shape[1:], BF16), pltpu.VMEM((total, width), BF16),
            pltpu.VMEM((total, width), F32), pltpu.VMEM((total, width), F32),
            pltpu.VMEM((256, total), BF16), pltpu.VMEM((256, total), F32),
            pltpu.VMEM((total, 256), F32), pltpu.VMEM((total, 256), BF16),
        ]
        + [pltpu.VMEM(du_shape, BF16), pltpu.VMEM(dd_shape, BF16)]
        + rooms(do_w.shape) + rooms(dq_shape)
        + [
            pltpu.VMEM((extra, do_w.shape[0] // 8, do_w.shape[1]), BF16),
            pltpu.VMEM((extra, dq_shape[0] // 8, dq_shape[1]), BF16),
            pltpu.VMEM((2, 1 + far, 8, width), F32), pltpu.VMEM((2, 4 + far, 8, width), F32),
            pltpu.SemaphoreType.DMA((2, 5)), pltpu.SemaphoreType.DMA((7,)), pltpu.SemaphoreType.DMA((4,)),
            pltpu.SemaphoreType.DMA((BACK_MESSAGES,)), pltpu.SemaphoreType.DMA((BACK_MESSAGES,)),
        ],
        compiler_params=pltpu.CompilerParams(
            vmem_limit_bytes=62 * 1024 * 1024, collective_id=1, has_side_effects=True
        ),
        name="back",
    )(tok, meta, gain1, tab, front_sums, qa, ka, va, do, x, gh, wq, du, dd, do_w)


def vectors_body(v, attn_gain, attn_shift, bias, freq, out_bias, mlp_gain, mlp_shift, up_bias, down_bias):
    cols = bias.shape[1]
    mlp_gain[...] = v[0, :]
    mlp_shift[...] = v[1, :]
    out_bias[...] = v[2, :]
    down_bias[...] = v[3, :]
    up_bias[...] = v[4, :]
    attn_gain[...] = v[19, :]
    attn_shift[...] = v[20, :]
    for n in range(3):
        bias[n : n + 1, :] = v[10:11, cols * n : cols * (n + 1)]
    first = [v[8:10, HEAD_DIM * n : HEAD_DIM * n + HALF] for n in range(cols // HEAD_DIM)]
    second = [v[8:10, HEAD_DIM * n + HALF : HEAD_DIM * (n + 1)] for n in range(cols // HEAD_DIM)]
    freq[...] = jnp.concatenate([a + b for a, b in zip(first, second)], axis=1)


def split_vectors(v, cols, units):
    width = v.shape[1]
    flat = lambda n: jax.ShapeDtypeStruct((n,), F32)
    return pl.pallas_call(
        vectors_body,
        out_shape=[
            flat(width), flat(width), jax.ShapeDtypeStruct((3, cols), F32), jax.ShapeDtypeStruct((2, cols // 2), F32),
            flat(width), flat(width), flat(width), flat(units), flat(width),
        ],
        in_specs=[VMEM],
        out_specs=[VMEM] * 9,
        name="vectors",
    )(v)


def body(
    n_dp, n_tensor, tokens, cotangent, kept_counts, patch_pos, attn_gain, attn_shift, qkv_weight, qkv_bias,
    rope_freq, out_weight, out_bias, mlp_gain, mlp_shift, up_weight, up_bias, down_weight, down_bias,
):
    width = tokens.shape[1]
    cols = qkv_weight.shape[2]
    groups = n_tensor
    wq = qkv_weight.reshape(width, 3 * cols)
    vectors = (qkv_bias, rope_freq, up_bias, attn_gain, attn_shift, out_bias, mlp_gain, mlp_shift, down_bias)
    qa, ka, va, do, block_out, gh, x, wq_all, tab, meta, dwo, piece_u, piece_d, sums = front(
        groups, n_dp, tokens, patch_pos, kept_counts, vectors, cotangent, wq, out_weight, up_weight, down_weight,
    )
    res = back(
        groups, n_dp, tokens, meta, attn_gain, tab, sums, qa, ka, va, do, x, gh, wq_all, piece_u, piece_d, dwo
    )
    grad_tokens, sums, du, dd, do_w, dq = res
    d_again, d_ashift, d_bias, d_freq, d_ob, d_mgain, d_mshift, d_ub, d_db = split_vectors(
        sums, cols, up_weight.shape[1]
    )
    return (
        block_out, grad_tokens, d_again, d_ashift, dq.reshape(width, 3, cols).astype(F32), d_bias, d_freq,
        do_w.astype(F32), d_ob, d_mgain, d_mshift, du.astype(F32), d_ub, dd.astype(F32), d_db,
    )


def solution(mesh):
    return jax.shard_map(
        functools.partial(body, mesh.shape["dp"], mesh.shape["tensor"]),
        mesh=mesh,
        in_specs=(
            P("dp", None), P("dp", None), P("dp"), P(None, "dp"), P(), P(), P(None, None, "tensor"),
            P(None, "tensor"), P(None, "tensor"), P("tensor", None), P(), P(), P(), P(None, "tensor"),
            P("tensor"), P("tensor", None), P(),
        ),
        out_specs=(
            P("dp", None), P("dp", None), P(), P(), P(None, None, "tensor"), P(None, "tensor"),
            P(None, "tensor"), P("tensor", None), P(), P(), P(), P(None, "tensor"), P("tensor"),
            P("tensor", None), P(),
        ),
        check_vma=False,
    )
```
